256 devices in a mesh: seq: 32 (over z_hi, x, core), fsdp: 8 (over z_lo, y).
Axes of the slice: x: 4, y: 4, z: 8 (z_hi: 4, z_lo: 2; z = z_hi * 2 + z_lo), core: 2. Of those that a mesh axis runs over, the one named last changes fastest.
Arguments:
- activations: bfloat16 [65536, 2048], P('seq', 'fsdp'), may hold values from -3 to 3
- mix_first: bfloat16 [256, 256], replicated, may hold values from -0.375 to 0.375
- twiddle: float32 [256, 256], P('seq'), may hold values from 0.4 to 2
- mix_second: bfloat16 [256, 256], replicated, may hold values from -0.375 to 0.375
- up_first: bfloat16 [8, 256, 256], P('fsdp'), may hold values from -0.375 to 0.375
- up_second: bfloat16 [8, 256, 1024], P('fsdp'), may hold values from -0.375 to 0.375
- down_first: bfloat16 [8, 1024, 256], P('fsdp'), may hold values from -0.1875 to 0.1875
- down_second: bfloat16 [8, 256, 256], P('fsdp'), may hold values from -0.375 to 0.375
- grad_out: bfloat16 [65536, 2048], P('seq', 'fsdp'), may hold values from -3 to 3
Outputs:
- output: bfloat16 [65536, 2048], P('seq', 'fsdp')
- grad_inputs: bfloat16 [65536, 2048], P('seq', 'fsdp')
- grad_up_first: float32 [8, 256, 256], P('fsdp')
- grad_up_second: float32 [8, 256, 1024], P('fsdp')
- grad_down_first: float32 [8, 1024, 256], P('fsdp')
- grad_down_second: float32 [8, 256, 256], P('fsdp')
The draws below stay inside these ranges and needn't reach their ends.
All inputs are finite; a program needn't handle non-finite values.
Results may differ from the reference program's by a relative error of at most 0.01.
Values may be sent and summed in bfloat16 or wider, within the bound.
A program may use at most 128 MiB of HBM per device.

```python
import math
import jax
import jax.numpy as jnp
from jax import lax

BLK = 256
D = 2048
FF = 8192
NBLK = 8
LENGTH = 65536


def shard_levels(key, extent, split, smallest, high):
    level, own = 1.0, jax.random.fold_in(key, 6)
    for dim, parts in split:
        heights = jnp.exp(jax.random.uniform(jax.random.fold_in(own, dim), (parts,), jnp.float32, smallest / len(split), high / len(split)))
        level = level * jnp.repeat(heights, extent[dim] // parts).reshape([-1 if axis == dim else 1 for axis in range(len(extent))])
    return level


def scatter_about(stream_key, shape, deviation, limit, pieces=(), kind=jnp.bfloat16):
    drawn = jax.random.normal(stream_key, shape, jnp.float32) * deviation
    if len(pieces) > 0:
        drawn = shard_levels(stream_key, shape, pieces, -0.22, 0.18) * drawn
    return jnp.clip(drawn, min=-limit, max=limit).astype(kind)


def setup_inputs(seed: int = 0) -> dict:
    key_of = jax.random.split(jax.random.key(seed), 10)
    activations = scatter_about(key_of[0], (LENGTH, D), 0.5, 3.0, ((0, 32), (1, 8)))
    mix_first = scatter_about(key_of[1], (BLK, BLK), BLK ** -0.5, 0.375)
    twiddle = jnp.clip(jnp.exp(math.log(2.0) - 1.609438 * jax.random.uniform(key_of[2], (BLK, BLK), jnp.float32) ** shard_levels(key_of[2], (BLK, BLK), ((0, 32),), -0.2, 0.2)), 0.4, 2.0)
    mix_second = scatter_about(key_of[3], (BLK, BLK), BLK ** -0.5, 0.375)
    up_first = scatter_about(key_of[4], (NBLK, D // NBLK, D // NBLK), (D // NBLK) ** -0.5, 0.375, ((0, 8),))
    up_second = scatter_about(key_of[5], (NBLK, D // NBLK, FF // NBLK), (D // NBLK) ** -0.5, 0.375, ((0, 8),))
    down_first = scatter_about(key_of[6], (NBLK, FF // NBLK, D // NBLK), (FF // NBLK) ** -0.5, 0.1875, ((0, 8),))
    down_second = scatter_about(key_of[7], (NBLK, D // NBLK, D // NBLK), (D // NBLK) ** -0.5, 0.375, ((0, 8),))
    grad_out = scatter_about(key_of[8], (LENGTH, D), 0.5, 3.0, ((0, 32), (1, 8)))
    return dict(activations=activations, mix_first=mix_first, twiddle=twiddle, mix_second=mix_second, up_first=up_first, up_second=up_second, down_first=down_first, down_second=down_second, grad_out=grad_out)


root_two_pi = 0.7978845608028654
cubic_term = 0.044715


def gelu_value(values):
    inner = root_two_pi * (values + cubic_term * values * values * values)
    return 0.5 * values * (1.0 + jnp.tanh(inner))


def gelu_slope(values):
    inner = root_two_pi * (values + cubic_term * values * values * values)
    hyper = jnp.tanh(inner)
    return 0.5 * (1.0 + hyper) + 0.5 * values * (1.0 - hyper * hyper) * root_two_pi * (1.0 + 3.0 * cubic_term * values * values)


def product(form, left, right):
    return jnp.einsum(form, left.astype(jnp.float32), right.astype(jnp.float32))


def permute_blocks(values):
    count, blocks, width = values.shape
    stride = width // blocks
    return jnp.transpose(values.reshape(count, blocks, blocks, stride), (0, 2, 3, 1)).reshape(count, blocks, width)


def unpermute_blocks(values):
    count, blocks, width = values.shape
    stride = width // blocks
    return jnp.transpose(values.reshape(count, blocks, stride, blocks), (0, 3, 1, 2)).reshape(count, blocks, width)


def mlp_block(hidden_rows, grad_rows, up_first, up_second, down_first, down_second):
    count = hidden_rows.shape[0]
    blocks, width = up_first.shape[0], up_first.shape[1]
    hidden_three = hidden_rows.reshape(count, blocks, width)
    up_mid = product("tkp,kpq->tkq", hidden_three, up_first).astype(jnp.bfloat16)
    up_perm = permute_blocks(up_mid)
    pre_act = product("tge,geo->tgo", up_perm, up_second)
    activated = gelu_value(pre_act).astype(jnp.bfloat16)
    down_mid = product("tgo,goq->tgq", activated, down_first).astype(jnp.bfloat16)
    down_perm = permute_blocks(down_mid)
    down_out = product("tge,geq->tgq", down_perm, down_second).reshape(count, blocks * width)
    output_rows = (hidden_rows.astype(jnp.float32) + down_out).astype(jnp.bfloat16)
    grad_three = grad_rows.reshape(count, blocks, width)
    sum_down_second = product("tge,tgq->geq", down_perm, grad_three)
    back_perm = product("tgq,geq->tge", grad_three, down_second).astype(jnp.bfloat16)
    back_mid = unpermute_blocks(back_perm)
    sum_down_first = product("tgo,tgq->goq", activated, back_mid)
    grad_act = product("tgq,goq->tgo", back_mid, down_first)
    grad_pre = (grad_act * gelu_slope(pre_act)).astype(jnp.bfloat16)
    sum_up_second = product("tge,tgo->geo", up_perm, grad_pre)
    grad_perm = product("tgo,geo->tge", grad_pre, up_second).astype(jnp.bfloat16)
    grad_mid = unpermute_blocks(grad_perm)
    sum_up_first = product("tkp,tkq->kpq", hidden_three, grad_mid)
    grad_inner = product("tkq,kpq->tkp", grad_mid, up_first).reshape(count, blocks * width)
    grad_hidden = (grad_rows.astype(jnp.float32) + grad_inner).astype(jnp.bfloat16)
    return output_rows, grad_hidden, (sum_up_first, sum_up_second, sum_down_first, sum_down_second)


def reference(activations, mix_first, twiddle, mix_second, up_first, up_second, down_first, down_second, grad_out):
    group = math.gcd(D, 128)
    count = D // group

    def split_groups(values):
        return jnp.moveaxis(values.reshape(BLK, BLK, count, group), 2, 0)

    def join_groups(values):
        return jnp.moveaxis(values, 0, 2).reshape(BLK * BLK, D)

    def forward_mix(portion):
        first_pass = (product("abc,bj->ajc", portion, mix_first) * twiddle[:, :, None]).astype(jnp.bfloat16)
        return product("ajc,ai->ijc", first_pass, mix_second).astype(jnp.bfloat16)

    mixed = join_groups(lax.map(forward_mix, split_groups(activations)))
    inputs_float = activations.astype(jnp.float32)
    gating = jax.nn.sigmoid(inputs_float)
    mixed_float = mixed.astype(jnp.float32)
    hidden = (inputs_float + gating * mixed_float).astype(jnp.bfloat16)

    rows_block = min(BLK * BLK, 2048)
    number = (BLK * BLK) // rows_block

    def scan_step(carry, inputs):
        output_rows, grad_rows, terms = mlp_block(inputs[0], inputs[1], up_first, up_second, down_first, down_second)
        carry = tuple(carry[index] + terms[index] for index in range(4))
        return carry, (output_rows, grad_rows)

    initial = (jnp.zeros(up_first.shape, jnp.float32), jnp.zeros(up_second.shape, jnp.float32),
               jnp.zeros(down_first.shape, jnp.float32), jnp.zeros(down_second.shape, jnp.float32))
    totals, stacked = lax.scan(scan_step, initial, (hidden.reshape(number, rows_block, D), grad_out.reshape(number, rows_block, D)))
    output = stacked[0].reshape(BLK * BLK, D)
    grad_hidden = stacked[1].reshape(BLK * BLK, D)
    grad_float = grad_hidden.astype(jnp.float32)
    grad_mixed = (grad_float * gating).astype(jnp.bfloat16)

    def backward_mix(portion):
        back_rows = product("ijc,ai->ajc", portion, mix_second).astype(jnp.bfloat16)
        twisted = (back_rows.astype(jnp.float32) * twiddle[:, :, None]).astype(jnp.bfloat16)
        return product("ajc,bj->abc", twisted, mix_first)

    mix_grad = join_groups(lax.map(backward_mix, split_groups(grad_mixed)))
    grad_inputs = (grad_float * (1.0 + gating * (1.0 - gating) * mixed_float) + mix_grad).astype(jnp.bfloat16)
    scale = 1.0 / BLK
    return (output, grad_inputs, totals[0] * scale, totals[1] * scale, totals[2] * scale, totals[3] * scale)
```

```python
import jax
import jax.numpy as jnp
from jax import lax
from jax.sharding import PartitionSpec as P

root_two_pi = 0.7978845608028654
cubic_term = 0.044715


def gelu_both(values):
    square = values * values
    hyper = jnp.tanh(root_two_pi * values * (1.0 + cubic_term * square))
    half = 0.5 * (1.0 + hyper)
    slope = half + 0.5 * values * (1.0 - hyper * hyper) * root_two_pi * (1.0 + 3.0 * cubic_term * square)
    return values * half, slope


def product(form, left, right):
    return jnp.einsum(form, left, right, preferred_element_type=jnp.float32)


def column_pass(field, factor):
    result = product(
        "ajc,ai->ijc", lax.all_to_all(field, "seq", split_axis=1, concat_axis=0, tiled=True), factor
    ).astype(jnp.bfloat16)
    return lax.all_to_all(result, "seq", split_axis=0, concat_axis=1, tiled=True)


def swap_blocks(rows):
    return lax.all_to_all(rows, "fsdp", split_axis=0, concat_axis=0, tiled=True)


def shards(activations, mix_first, twiddle, mix_second, up_first, up_second, down_first, down_second, grad_out):
    bf16 = jnp.bfloat16
    local_rows, local_channels = activations.shape
    block_rows = twiddle.shape[0]
    length = mix_first.shape[0]
    width = up_first.shape[1]
    units = up_second.shape[2]
    blocks = lax.axis_size("fsdp")
    members = lax.axis_size("seq")
    stride = width // blocks
    first, second, third, fourth = up_first[0], up_second[0], down_first[0], down_second[0]
    second = second.reshape(stride, blocks, units).transpose(1, 0, 2).reshape(width, units)
    fourth = fourth.reshape(stride, blocks, width).transpose(1, 0, 2).reshape(width, width)
    back_mid = swap_blocks(product("tq,eq->et", grad_out, fourth).astype(bf16))

    inputs_three = activations.reshape(block_rows, length, local_channels)
    first_pass = (product("abc,bj->ajc", inputs_three, mix_first) * twiddle[:, :, None]).astype(bf16)
    mixed = column_pass(first_pass, mix_second).reshape(local_rows, local_channels)
    inputs_float = activations.astype(jnp.float32)
    gating = jax.nn.sigmoid(inputs_float)
    mixed_float = mixed.astype(jnp.float32)
    hidden = (inputs_float + gating * mixed_float).astype(bf16)

    up_perm = swap_blocks(product("tp,pq->qt", hidden, first).astype(bf16))
    pre_act = product("eo,et->ot", second, up_perm)
    value, slope = gelu_both(pre_act)
    activated = value.astype(bf16)
    down_perm = swap_blocks(product("oq,ot->qt", third, activated).astype(bf16))
    output = (hidden.astype(jnp.float32) + product("et,eq->tq", down_perm, fourth)).astype(bf16)
    grad_pre = (product("oq,qt->ot", third, back_mid) * slope).astype(bf16)
    grad_mid = swap_blocks(product("eo,ot->et", second, grad_pre).astype(bf16))
    grad_inner = product("qt,pq->tp", grad_mid, first)
    grad_hidden = (grad_out.astype(jnp.float32) + grad_inner).astype(bf16)

    terms = jnp.concatenate(
        (
            product("qt,tp->qp", grad_mid, hidden).astype(bf16),
            product("ot,et->oe", grad_pre, up_perm).astype(bf16),
            product("ot,qt->oq", activated, back_mid).astype(bf16),
            product("et,tq->eq", down_perm, grad_out).astype(bf16),
        )
    )
    terms = lax.all_to_all(terms, "seq", split_axis=0, concat_axis=0, tiled=True)
    owned = jnp.sum(terms.reshape(members, -1, width).astype(jnp.float32), axis=0).astype(bf16)
    totals = lax.all_gather(owned, "seq", axis=0, tiled=True).astype(jnp.float32) * (1.0 / length)

    grad_float = grad_hidden.astype(jnp.float32)
    grad_mixed = (grad_float * gating).astype(bf16)
    back_rows = column_pass(grad_mixed.reshape(block_rows, length, local_channels), mix_second.T)
    twisted = (back_rows.astype(jnp.float32) * twiddle[:, :, None]).astype(bf16)
    mix_grad = product("ajc,bj->abc", twisted, mix_first).reshape(local_rows, local_channels)
    grad_inputs = (grad_float * (1.0 + gating * (1.0 - gating) * mixed_float) + mix_grad).astype(bf16)

    sum_first = totals[:width].T
    sum_second = totals[width : width + units].T.reshape(blocks, stride, units).transpose(1, 0, 2).reshape(width, units)
    sum_third = totals[width + units : width + 2 * units]
    sum_fourth = totals[width + 2 * units :].reshape(blocks, stride, width).transpose(1, 0, 2).reshape(width, width)
    return (output, grad_inputs, sum_first[None], sum_second[None], sum_third[None], sum_fourth[None])


def solution(mesh):
    block = P("fsdp", None, None)
    in_specs = (P("seq", "fsdp"), P(), P("seq", None), P(), block, block, block, block, P("seq", "fsdp"))
    out_specs = (P("seq", "fsdp"), P("seq", "fsdp"), block, block, block, block)
    return jax.shard_map(shards, mesh=mesh, in_specs=in_specs, out_specs=out_specs, check_vma=False)
```

```python
import functools

import jax
import jax.numpy as jnp
from jax import lax
from jax.experimental import pallas as pl
from jax.experimental.pallas import tpu as pltpu
from jax.sharding import PartitionSpec as P

MESH = pl.DeviceIdType.MESH
bf16, f32 = jnp.bfloat16, jnp.float32
root_two_pi = 0.7978845608028654
cubic_term = 0.044715
CHUNKS = 2
A1, A2, A3, A4 = range(4)
BACK, UP, GRAD, DOWN = range(4)


def gelu_both(values):
    square = values * values
    hyper = jnp.tanh(root_two_pi * values * (1.0 + cubic_term * square))
    half = 0.5 * (1.0 + hyper)
    slope = half + 0.5 * values * (1.0 - hyper * hyper) * root_two_pi * (1.0 + 3.0 * cubic_term * square)
    return values * half, slope


def nn(left, right):
    return lax.dot_general(left, right, (((1,), (0,)), ((), ())), preferred_element_type=f32)


def nt(left, right):
    return lax.dot_general(left, right, (((1,), (1,)), ((), ())), preferred_element_type=f32)


def tn(left, right):
    return lax.dot_general(left, right, (((0,), (0,)), ((), ())), preferred_element_type=f32)


def layer(
    act_rows, act, gout, mix_in, mix_out, mix_fwd, mix_bwd, tw,
    first_t, second, second_t, third, third_t, fourth,
    out, grad_in, total,
    wide, extra, field_s, field_r, swap_s, swap_r, hidden, active, gpre, acc, send_terms, half_in, half_sum,
    quarter_in, quarter_sum, last_in,
    seq_send, seq_recv, swap_send, swap_recv, red_send, red_recv,
):
    s = lax.axis_index("seq")
    f = lax.axis_index("fsdp")
    zh, xx, core = s // 8, (s // 2) % 4, s % 2
    zl, yy = f // 4, f % 4
    rows = field_s.shape[3]
    span = swap_s.shape[3]

    def seq_peer(dz, n):
        return ((zh + dz) % 4 * 4 + (xx + n // 2) % 4) * 2 + (core + n) % 2

    def swap_peer(n):
        return (zl + n // 4) % 2 * 4 + (yy + n) % 4

    barrier = pltpu.get_barrier_semaphore()

    def greet(peer_seq, peer_fsdp):
        pl.semaphore_signal(barrier, inc=1, device_id={"seq": peer_seq, "fsdp": peer_fsdp}, device_id_type=MESH)

    @pl.loop(1, 32)
    def _(n):
        greet((s + n) % 32, f)

    @pl.loop(1, 8)
    def _(n):
        greet(s, (f + n) % 8)

    def seq_start(phase, q):
        pltpu.make_async_copy(field_s.at[phase, q, s], field_r.at[phase, q, s], seq_recv.at[phase, q]).start()
        for dz in (2, 1, 3, 0):
            @pl.loop(1 if dz == 0 else 0, 8)
            def _(n):
                peer = seq_peer(dz, n)
                pltpu.make_async_remote_copy(
                    src_ref=field_s.at[phase, q, peer], dst_ref=field_r.at[phase, q, s],
                    send_sem=seq_send.at[phase, q], recv_sem=seq_recv.at[phase, q],
                    device_id={"seq": peer, "fsdp": f}, device_id_type=MESH,
                ).start()

    def seq_wait(phase, q):
        whole = field_r.at[phase, q]
        pltpu.make_async_copy(whole, whole, seq_recv.at[phase, q]).wait()

    def swap_start(phase, q):
        own = pl.ds(pl.multiple_of(f * 32, 32), 32)
        pltpu.make_async_copy(swap_s.at[phase, q, own], swap_r.at[phase, q, own], swap_recv.at[phase, q]).start()

        @pl.loop(1, 8)
        def _(n):
            peer = swap_peer(8 - n)
            pltpu.make_async_remote_copy(
                src_ref=swap_s.at[phase, q, pl.ds(pl.multiple_of(peer * 32, 32), 32)], dst_ref=swap_r.at[phase, q, own],
                send_sem=swap_send.at[phase, q], recv_sem=swap_recv.at[phase, q],
                device_id={"seq": s, "fsdp": peer}, device_id_type=MESH,
            ).start()

    def swap_wait(phase, q):
        whole = swap_r.at[phase, q]
        pltpu.make_async_copy(whole, whole, swap_recv.at[phase, q]).wait()

    for a in range(8):
        lines = nn(mix_in[...], act_rows[a]) * tw[:, a : a + 1]
        for half in range(2):
            wide[half, pl.ds(a, 256, stride=8), :] = lines[:, half * 128 : half * 128 + 128]
    for q in range(CHUNKS):
        @pl.loop(0, 32)
        def _(d):
            for half in range(2):
                place = pl.ds(pl.multiple_of(q * 32 * rows + d * rows, 8), rows)
                field_s[A1, q, d, :, half * 128 : half * 128 + 128] = wide[half, place, :].astype(bf16)

    pl.semaphore_wait(barrier, 38)
    for q in range(CHUNKS):
        seq_start(A1, q)

    tile = 256
    tiles = span // tile

    def token_tile(t):
        return pl.ds(pl.multiple_of(t * tile, tile), tile)

    def field_tile(ref, phase, q, t):
        per = tile // rows
        return ref.at[phase, q, pl.ds(t * per, per)]

    for q in range(CHUNKS):
        @pl.loop(0, tiles)
        def _(t):
            swap_s[BACK, q, :, token_tile(t)] = nt(fourth[...], gout[q, token_tile(t), :]).astype(bf16)
        swap_start(BACK, q)

    def mix_columns(source, target, factor, q):
        for pair in range(rows // 16):
            part = pl.ds(pair * 16, 16)
            block = field_r[source, q, :, part, :].astype(f32).reshape(32, 2, 8, 256)
            mixed = [nn(factor[...], block[:, k].reshape(256, 256).astype(bf16)).reshape(32, 8, 256) for k in range(2)]
            field_s[target, q, :, part, :] = jnp.stack(mixed, axis=1).reshape(32, 16, 256).astype(bf16)

    def gate(q, t):
        return act[q, token_tile(t), :].astype(f32)

    for q in range(CHUNKS):
        seq_wait(A1, q)
        mix_columns(A1, A2, mix_fwd, q)
        seq_start(A2, q)

    for q in range(CHUNKS):
        seq_wait(A2, q)

        @pl.loop(0, tiles)
        def _(t):
            inputs = gate(q, t)
            mixed = field_tile(field_r, A2, q, t)[...].reshape(tile, 256).astype(f32)
            rows_hidden = (inputs + jax.nn.sigmoid(inputs) * mixed).astype(bf16)
            hidden[q, token_tile(t), :] = rows_hidden
            swap_s[UP, q, :, token_tile(t)] = nt(first_t[...], rows_hidden).astype(bf16)
        swap_start(UP, q)

    for q in range(CHUNKS):
        if q == 0:
            for other in range(CHUNKS):
                swap_wait(BACK, other)
        swap_wait(UP, q)

        @pl.loop(0, tiles)
        def _(t):
            columns = token_tile(t)
            up = swap_r[UP, q, :, columns]
            back = swap_r[BACK, q, :, columns]

            @pl.loop(0, 4)
            def _(o):
                units = pl.ds(pl.multiple_of(o * 256, 256), 256)
                value, slope = gelu_both(nn(second_t[units, :], up))
                active[q, units, columns] = value.astype(bf16)
                gpre[q, units, columns] = (nn(third[units, :], back) * slope).astype(bf16)
            swap_s[GRAD, q, :, columns] = nn(second[...], gpre[q, :, columns]).astype(bf16)
            swap_s[DOWN, q, :, columns] = nn(third_t[...], active[q, :, columns]).astype(bf16)
        swap_start(GRAD, q)
        swap_start(DOWN, q)

    for q in range(CHUNKS):
        swap_wait(GRAD, q)

        @pl.loop(0, tiles)
        def _(t):
            columns = token_tile(t)
            inner = tn(swap_r[GRAD, q, :, columns], first_t[...])
            back = (gout[q, columns, :].astype(f32) + inner).astype(bf16).astype(f32)
            gating = jax.nn.sigmoid(gate(q, t))
            mixed = field_tile(field_r, A2, q, t)[...].reshape(tile, 256).astype(f32)
            field_tile(field_s, A3, q, t)[...] = (back * gating).astype(bf16).reshape(tile // rows, rows, 256)
            rest = back * (1.0 + gating * (1.0 - gating) * mixed)
            for half in range(2):
                place = pl.ds(pl.multiple_of(q * span + t * tile, tile), tile)
                extra[half, place, :] = rest[:, half * 128 : half * 128 + 128]
        seq_start(A3, q)

    def add(place, values, q):
        if q == 0:
            acc[place, :] = values
        else:
            acc[place, :] += values

    for q in range(CHUNKS):
        @pl.loop(0, 4)
        def _(o):
            units = pl.ds(pl.multiple_of(o * 256, 256), 256)
            add(pl.ds(pl.multiple_of(256 + o * 256, 256), 256), nt(gpre[q, units, :], swap_r[UP, q]), q)
            add(pl.ds(pl.multiple_of(1280 + o * 256, 256), 256), nt(active[q, units, :], swap_r[BACK, q]), q)
        add(pl.ds(0, 256), nn(swap_r[GRAD, q], hidden[q]), q)

    for q in range(CHUNKS):
        swap_wait(DOWN, q)

        @pl.loop(0, tiles)
        def _(t):
            columns = token_tile(t)
            out[q, columns, :] = (hidden[q, columns, :].astype(f32) + tn(swap_r[DOWN, q, :, columns], fourth[...])).astype(bf16)
        add(pl.ds(2304, 256), nn(swap_r[DOWN, q], gout[q]), q)

    def core_peer():
        return {"seq": zh * 8 + xx * 2 + 1 - core, "fsdp": f}

    def x_peer(n):
        return {"seq": zh * 8 + (xx + n) % 4 * 2 + core, "fsdp": f}

    def z_peer(n):
        return {"seq": (zh + n) % 4 * 8 + xx * 2 + core, "fsdp": f}

    def red(stage, n, source, target, peer):
        return pltpu.make_async_remote_copy(
            src_ref=source, dst_ref=target, send_sem=red_send.at[stage, n], recv_sem=red_recv.at[stage, n],
            device_id=peer, device_id_type=MESH,
        )

    def rows_at(ref, start, count):
        return ref.at[pl.ds(pl.multiple_of(start, 16), count)]

    def reduce_core():
        @pl.loop(0, 10)
        def _(t):
            place = pl.ds(pl.multiple_of((1 - core) * 1280 + t * 128, 128), 128)
            send_terms[pl.ds(pl.multiple_of(t * 128, 128), 128), :] = acc[place, :].astype(bf16)
        copy = red(0, 0, send_terms, half_in, core_peer())
        copy.start()
        return [copy]

    def reduce_x():
        @pl.loop(0, 10)
        def _(t):
            place = pl.ds(pl.multiple_of(t * 128, 128), 128)
            own = acc[pl.ds(pl.multiple_of(core * 1280 + t * 128, 128), 128), :]
            half_sum[place, :] = (own + half_in[place, :].astype(f32)).astype(bf16)
        copies = [red(1, n - 1, rows_at(half_sum, (xx + n) % 4 * 320, 320), quarter_in.at[n - 1], x_peer(n)) for n in (2, 1, 3)]
        for copy in copies:
            copy.start()
        return copies

    def reduce_z():
        own = rows_at(half_sum, xx * 320, 320)[...].astype(f32)
        for n in range(3):
            own += quarter_in[n].astype(f32)
        quarter_sum[...] = own.astype(bf16)
        copies = [red(2, n - 1, rows_at(quarter_sum, (zh + n) % 4 * 80, 80), last_in.at[n - 1], z_peer(n)) for n in (2, 1, 3)]
        for copy in copies:
            copy.start()
        return copies

    def gather_z():
        own = rows_at(quarter_sum, zh * 80, 80)[...].astype(f32)
        for n in range(3):
            own += last_in[n].astype(f32)
        place = rows_at(total, core * 1280 + xx * 320 + zh * 80, 80)
        place[...] = own.astype(bf16)
        copies = [red(3, n - 1, place, place, z_peer(n)) for n in (2, 1, 3)]
        for copy in copies:
            copy.start()
        return copies

    def gather_x():
        place = rows_at(total, core * 1280 + xx * 320, 320)
        copies = [red(4, n - 1, place, place, x_peer(n)) for n in (2, 1, 3)]
        for copy in copies:
            copy.start()
        return copies

    def gather_core():
        place = rows_at(total, core * 1280, 1280)
        copy = red(5, 0, place, place, core_peer())
        copy.start()
        return [copy]

    def finish(copies):
        for copy in copies:
            copy.wait()

    copies = reduce_core()
    for q in range(CHUNKS):
        seq_wait(A3, q)
        mix_columns(A3, A4, mix_bwd, q)
        seq_start(A4, q)
        if q == 0:
            finish(copies)
            copies = reduce_x()
    finish(copies)
    finish(reduce_z())
    finish(gather_z())
    finish(gather_x())
    copies = gather_core()

    for q in range(CHUNKS):
        seq_wait(A4, q)

        @pl.loop(0, 32)
        def _(d):
            for half in range(2):
                place = pl.ds(pl.multiple_of(q * 32 * rows + d * rows, 8), rows)
                wide[half, place, :] = field_r[A4, q, d, :, half * 128 : half * 128 + 128].astype(f32)
    for a in range(8):
        lines = pl.ds(a, 256, stride=8)
        for half in range(2):
            twisted = (wide[half, lines, :] * tw[:, a : a + 1]).astype(bf16)
            grad_in[a, :, half * 128 : half * 128 + 128] = (extra[half, lines, :] + nn(mix_out[...], twisted)).astype(bf16)
    finish(copies)

    for q in range(CHUNKS):
        for phase in range(4):
            sent = field_s.at[phase, q, pl.ds(0, 31)]
            pltpu.make_async_copy(sent, sent, seq_send.at[phase, q]).wait()
            sent = swap_s.at[phase, q, pl.ds(0, 224)]
            pltpu.make_async_copy(sent, sent, swap_send.at[phase, q]).wait()


def shards(activations, mix_first, twiddle, mix_second, up_first, up_second, down_first, down_second, grad_out):
    per = 8 // CHUNKS
    span = 2048 // CHUNKS
    first, second, third, fourth = up_first[0], up_second[0], down_first[0], down_second[0]
    second = second.reshape(32, 8, 1024).transpose(1, 0, 2).reshape(256, 1024)
    fourth = fourth.reshape(32, 8, 256).transpose(1, 0, 2).reshape(256, 256)

    def reorder(values):
        return values.reshape(32, CHUNKS, per, -1).transpose(1, 0, 2, 3).reshape(256, -1)

    def token_order(values):
        return values.reshape(8, 32, CHUNKS, per, 256).transpose(2, 1, 3, 0, 4).reshape(CHUNKS, span, 256)

    mix_in = reorder(mix_first.T)
    mix_out = reorder(reorder(mix_first).T).T
    tw = reorder(twiddle.T)
    act_rows = activations.reshape(8, 256, 256)
    args = (
        act_rows, token_order(activations), token_order(grad_out), mix_in, mix_out, mix_second.T, mix_second, tw,
        first.T, second, second.T, third, third.T, fourth,
    )
    vmem = pl.BlockSpec(memory_space=pltpu.VMEM)
    rows = 64 // CHUNKS
    output, grad_in, total = pl.pallas_call(
        layer,
        name="monarch_layer",
        out_shape=(
            jax.ShapeDtypeStruct((CHUNKS, span, 256), bf16),
            jax.ShapeDtypeStruct((8, 256, 256), bf16),
            jax.ShapeDtypeStruct((2560, 256), bf16),
        ),
        in_specs=[vmem] * len(args),
        out_specs=(vmem,) * 3,
        scratch_shapes=[
            pltpu.VMEM((2, 2048, 128), f32),
            pltpu.VMEM((2, 2048, 128), f32),
            pltpu.VMEM((4, CHUNKS, 32, rows, 256), bf16),
            pltpu.VMEM((4, CHUNKS, 32, rows, 256), bf16),
            pltpu.VMEM((4, CHUNKS, 256, span), bf16),
            pltpu.VMEM((4, CHUNKS, 256, span), bf16),
            pltpu.VMEM((CHUNKS, span, 256), bf16),
            pltpu.VMEM((CHUNKS, 1024, span), bf16),
            pltpu.VMEM((CHUNKS, 1024, span), bf16),
            pltpu.VMEM((2560, 256), f32),
            pltpu.VMEM((1280, 256), bf16),
            pltpu.VMEM((1280, 256), bf16),
            pltpu.VMEM((1280, 256), bf16),
            pltpu.VMEM((3, 320, 256), bf16),
            pltpu.VMEM((320, 256), bf16),
            pltpu.VMEM((3, 80, 256), bf16),
            pltpu.SemaphoreType.DMA((4, CHUNKS)),
            pltpu.SemaphoreType.DMA((4, CHUNKS)),
            pltpu.SemaphoreType.DMA((4, CHUNKS)),
            pltpu.SemaphoreType.DMA((4, CHUNKS)),
            pltpu.SemaphoreType.DMA((6, 3)),
            pltpu.SemaphoreType.DMA((6, 3)),
        ],
        compiler_params=pltpu.CompilerParams(collective_id=0, has_side_effects=True, vmem_limit_bytes=60 << 20),
    )(*args)

    output = output.reshape(CHUNKS, 32, per, 8, 256).transpose(3, 1, 0, 2, 4).reshape(2048, 256)
    grad_in = grad_in.reshape(8, CHUNKS, 32, per, 256).transpose(0, 2, 1, 3, 4).reshape(2048, 256)
    totals = total.astype(f32) * (1.0 / 256)
    sum_first = totals[:256].T
    sum_second = totals[256:1280].T.reshape(8, 32, 1024).transpose(1, 0, 2).reshape(256, 1024)
    sum_third = totals[1280:2304]
    sum_fourth = totals[2304:].reshape(8, 32, 256).transpose(1, 0, 2).reshape(256, 256)
    return (output, grad_in, sum_first[None], sum_second[None], sum_third[None], sum_fourth[None])


def solution(mesh):
    block = P("fsdp", None, None)
    in_specs = (P("seq", "fsdp"), P(), P("seq", None), P(), block, block, block, block, P("seq", "fsdp"))
    out_specs = (P("seq", "fsdp"), P("seq", "fsdp"), block, block, block, block)
    return jax.shard_map(shards, mesh=mesh, in_specs=in_specs, out_specs=out_specs, check_vma=False)
```

```python
import functools

import jax
import jax.numpy as jnp
from jax import lax
from jax.experimental import pallas as pl
from jax.experimental.pallas import tpu as pltpu
from jax.sharding import PartitionSpec as P

MESH = pl.DeviceIdType.MESH
bf16, f32 = jnp.bfloat16, jnp.float32
root_two_pi = 0.7978845608028654
cubic_term = 0.044715
CHUNKS = 4
A1, A2, A3, A4 = range(4)
BACK, UP, GRAD, DOWN = range(4)


def gelu_both(values):
    square = values * values
    hyper = jnp.tanh(root_two_pi * values * (1.0 + cubic_term * square))
    half = 0.5 * (1.0 + hyper)
    slope = half + 0.5 * values * (1.0 - hyper * hyper) * root_two_pi * (1.0 + 3.0 * cubic_term * square)
    return values * half, slope


def nn(left, right):
    return lax.dot_general(left, right, (((1,), (0,)), ((), ())), preferred_element_type=f32)


def nt(left, right):
    return lax.dot_general(left, right, (((1,), (1,)), ((), ())), preferred_element_type=f32)


def tn(left, right):
    return lax.dot_general(left, right, (((0,), (0,)), ((), ())), preferred_element_type=f32)


def layer(
    act_rows, mix_first, twiddle, gout_any, mix_second_any, first_any, second_any, third_any, fourth_any,
    out, tall_out, broad_out, grad_in,
    gout_rows, mix_bwd, first, second_raw, third, fourth_raw,
    act, gout, mix_fwd, first_t, second, second_t, third_t, fourth, total, out_v, tall_v, broad_v,
    wide, extra, field_s, field_r, swap_s, swap_r, hidden, active, gpre, acc, send_terms, half_in, half_sum,
    quarter_in, quarter_sum, last_in,
    seq_send, seq_recv, swap_send, swap_recv, red_send, red_recv, load_sem, store_sem,
):
    s = lax.axis_index("seq")
    f = lax.axis_index("fsdp")
    zh, xx, core = s // 8, (s // 2) % 4, s % 2
    zl, yy = f // 4, f % 4
    rows = field_s.shape[3]
    span = swap_s.shape[3]

    def seq_peer(dz, n):
        return ((zh + dz) % 4 * 4 + (xx + n // 2) % 4) * 2 + (core + n) % 2

    def swap_peer(n):
        return (zl + n // 4) % 2 * 4 + (yy + n) % 4

    barrier = pltpu.get_barrier_semaphore()

    def greet(peer_seq, peer_fsdp):
        pl.semaphore_signal(barrier, inc=1, device_id={"seq": peer_seq, "fsdp": peer_fsdp}, device_id_type=MESH)

    @pl.loop(1, 32)
    def _(n):
        greet((s + n) % 32, f)

    @pl.loop(1, 8)
    def _(n):
        greet(s, (f + n) % 8)

    def seq_start(phase, q, planes=(2, 1, 3, 0)):
        if 0 in planes:
            pltpu.make_async_copy(field_s.at[phase, q, s], field_r.at[phase, q, s], seq_recv.at[phase, q]).start()
        for dz in planes:
            @pl.loop(1 if dz == 0 else 0, 8)
            def _(n):
                peer = seq_peer(dz, n)
                pltpu.make_async_remote_copy(
                    src_ref=field_s.at[phase, q, peer], dst_ref=field_r.at[phase, q, s],
                    send_sem=seq_send.at[phase, q], recv_sem=seq_recv.at[phase, q],
                    device_id={"seq": peer, "fsdp": f}, device_id_type=MESH,
                ).start()

    def seq_wait(phase, q):
        whole = field_r.at[phase, q]
        pltpu.make_async_copy(whole, whole, seq_recv.at[phase, q]).wait()

    def swap_start(phase, q):
        own = pl.ds(pl.multiple_of(f * 32, 32), 32)
        pltpu.make_async_copy(swap_s.at[phase, q, own], swap_r.at[phase, q, own], swap_recv.at[phase, q]).start()

        @pl.loop(1, 8)
        def _(n):
            peer = swap_peer(8 - n)
            pltpu.make_async_remote_copy(
                src_ref=swap_s.at[phase, q, pl.ds(pl.multiple_of(peer * 32, 32), 32)], dst_ref=swap_r.at[phase, q, own],
                send_sem=swap_send.at[phase, q], recv_sem=swap_recv.at[phase, q],
                device_id={"seq": s, "fsdp": peer}, device_id_type=MESH,
            ).start()

    def swap_wait(phase, q):
        whole = swap_r.at[phase, q]
        pltpu.make_async_copy(whole, whole, swap_recv.at[phase, q]).wait()

    loads = [
        pltpu.make_async_copy(source, target, load_sem.at[index])
        for index, (source, target) in enumerate((
            (gout_any, gout_rows), (fourth_any, fourth_raw), (mix_second_any, mix_bwd),
            (first_any, first), (second_any, second_raw), (third_any, third),
        ))
    ]
    for load in loads:
        load.start()

    row = lax.broadcasted_iota(jnp.int32, (256, 256), 0)
    column = lax.broadcasted_iota(jnp.int32, (256, 256), 1)
    one, zero = jnp.ones((256, 256), f32), jnp.zeros((256, 256), f32)
    eye = jnp.where(row == column, one, zero).astype(bf16)
    sort = jnp.where(column == (row % 32) * 8 + row // 32, one, zero).astype(bf16)
    unsort = jnp.where(row == (column % 32) * 8 + column // 32, one, zero).astype(bf16)

    def flip(values):
        return nt(eye, values).astype(bf16)

    def halves(values):
        return [(half, values[:, half * 128 : half * 128 + 128]) for half in range(2)]

    def interleave(index, values):
        for half, part in halves(values):
            wide[half, pl.ds(index, 256, stride=8), :] = part

    def block_place(d, q):
        return pl.ds(pl.multiple_of(d * 64 + q * rows, 8), rows)

    tw = twiddle[...].T
    mix_in = flip(mix_first[...])
    for a in range(8):
        interleave(a, nn(mix_in, act_rows[a]) * tw[:, a : a + 1])
    for q in range(CHUNKS):
        @pl.loop(0, 32)
        def _(d):
            for half in range(2):
                field_s[A1, q, d, :, half * 128 : half * 128 + 128] = wide[half, block_place(d, q), :].astype(bf16)

    pl.semaphore_wait(barrier, 38)
    for q in range(CHUNKS):
        seq_start(A1, q)

    tile = 256
    tiles = span // tile
    per = tile // rows

    def token_tile(t):
        return pl.ds(pl.multiple_of(t * tile, tile), tile)

    def field_tile(ref, phase, q, t):
        return ref.at[phase, q, pl.ds(t * per, per)]

    def token_order(source, target):
        for a in range(8):
            interleave(a, source[a].astype(f32))
        for q in range(CHUNKS):
            @pl.loop(0, 32)
            def _(d):
                place = pl.ds(pl.multiple_of(d * rows, rows), rows)
                for half in range(2):
                    target[q, place, half * 128 : half * 128 + 128] = wide[half, block_place(d, q), :].astype(bf16)

    def scatter(target, q, t, values):
        for half, part in halves(values):
            for n in range(per):
                target[half, block_place(t * per + n, q), :] = part[n * rows : (n + 1) * rows]

    loads[0].wait()
    token_order(gout_rows, gout)
    loads[1].wait()
    fourth[...] = nn(sort, fourth_raw[...]).astype(bf16)
    for q in range(CHUNKS):
        @pl.loop(0, tiles)
        def _(t):
            swap_s[BACK, q, :, token_tile(t)] = nt(fourth[...], gout[q, token_tile(t), :]).astype(bf16)
        swap_start(BACK, q)
    token_order(act_rows, act)
    for load in loads[2:]:
        load.wait()
    mix_fwd[...] = flip(mix_bwd[...])
    first_t[...] = flip(first[...])
    for o in range(4):
        units = pl.ds(o * 256, 256)
        sorted_units = nn(sort, second_raw[:, units]).astype(bf16)
        second[:, units] = sorted_units
        second_t[units, :] = flip(sorted_units)
        third_t[:, units] = flip(third[units, :])

    def mix_columns(source, target, factor, q):
        for pair in range(rows // 16):
            part = pl.ds(pair * 16, 16)
            block = field_r[source, q, :, part, :].astype(f32).reshape(32, 2, 8, 256)
            mixed = [nn(factor[...], block[:, k].reshape(256, 256).astype(bf16)).reshape(32, 8, 256) for k in range(2)]
            field_s[target, q, :, part, :] = jnp.stack(mixed, axis=1).reshape(32, 16, 256).astype(bf16)

    def gate(q, t):
        return act[q, token_tile(t), :].astype(f32)

    for q in range(CHUNKS):
        seq_wait(A1, q)
        mix_columns(A1, A2, mix_fwd, q)
        seq_start(A2, q)

    for q in range(CHUNKS):
        seq_wait(A2, q)

        @pl.loop(0, tiles)
        def _(t):
            inputs = gate(q, t)
            mixed = field_tile(field_r, A2, q, t)[...].reshape(tile, 256).astype(f32)
            rows_hidden = (inputs + jax.nn.sigmoid(inputs) * mixed).astype(bf16)
            hidden[q, token_tile(t), :] = rows_hidden
            swap_s[UP, q, :, token_tile(t)] = nt(first_t[...], rows_hidden).astype(bf16)
        swap_start(UP, q)

    def add(place, values, q):
        if q == 0:
            acc[place, :] = values
        else:
            acc[place, :] += values

    for q in range(CHUNKS):
        if q == 0:
            for other in range(CHUNKS):
                swap_wait(BACK, other)
        swap_wait(UP, q)

        @pl.loop(0, tiles)
        def _(t):
            columns = token_tile(t)
            up = swap_r[UP, q, :, columns]
            back = swap_r[BACK, q, :, columns]

            @pl.loop(0, 4)
            def _(o):
                units = pl.ds(pl.multiple_of(o * 256, 256), 256)
                value, slope = gelu_both(nn(second_t[units, :], up))
                active[q, units, columns] = value.astype(bf16)
                gpre[q, units, columns] = (nn(third[units, :], back) * slope).astype(bf16)
            swap_s[GRAD, q, :, columns] = nn(second[...], gpre[q, :, columns]).astype(bf16)
        swap_start(GRAD, q)

        @pl.loop(0, tiles)
        def _(t):
            columns = token_tile(t)
            swap_s[DOWN, q, :, columns] = nn(third_t[...], active[q, :, columns]).astype(bf16)
        swap_start(DOWN, q)

        @pl.loop(0, 4)
        def _(o):
            units = pl.ds(pl.multiple_of(o * 256, 256), 256)
            add(pl.ds(pl.multiple_of(256 + o * 256, 256), 256), nt(gpre[q, units, :], swap_r[UP, q]), q)
            add(pl.ds(pl.multiple_of(1280 + o * 256, 256), 256), nt(active[q, units, :], swap_r[BACK, q]), q)

    def back_rows(q):
        swap_wait(GRAD, q)

        @pl.loop(0, tiles)
        def _(t):
            columns = token_tile(t)
            inner = tn(swap_r[GRAD, q, :, columns], first_t[...])
            back = (gout[q, columns, :].astype(f32) + inner).astype(bf16).astype(f32)
            gating = jax.nn.sigmoid(gate(q, t))
            mixed = field_tile(field_r, A2, q, t)[...].reshape(tile, 256).astype(f32)
            field_tile(field_s, A3, q, t)[...] = (back * gating).astype(bf16).reshape(per, rows, 256)
            rest = back * (1.0 + gating * (1.0 - gating) * mixed)
            scatter(extra, q, t, rest)

    def out_rows(q):
        @pl.loop(0, tiles)
        def _(t):
            columns = token_tile(t)
            scatter(wide, q, t, hidden[q, columns, :].astype(f32) + tn(swap_r[DOWN, q, :, columns], fourth[...]))

    def last_terms(q):
        add(pl.ds(0, 256), nn(swap_r[GRAD, q], hidden[q]), q)
        swap_wait(DOWN, q)
        add(pl.ds(2304, 256), nn(swap_r[DOWN, q], gout[q]), q)

    def core_peer():
        return {"seq": zh * 8 + xx * 2 + 1 - core, "fsdp": f}

    def x_peer(n):
        return {"seq": zh * 8 + (xx + n) % 4 * 2 + core, "fsdp": f}

    def z_peer(n):
        return {"seq": (zh + n) % 4 * 8 + xx * 2 + core, "fsdp": f}

    def red(stage, n, source, target, peer):
        return pltpu.make_async_remote_copy(
            src_ref=source, dst_ref=target, send_sem=red_send.at[stage, n], recv_sem=red_recv.at[stage, n],
            device_id=peer, device_id_type=MESH,
        )

    def rows_at(ref, start, count):
        return ref.at[pl.ds(pl.multiple_of(start, 16), count)]

    def reduce_core():
        @pl.loop(0, 10)
        def _(t):
            place = pl.ds(pl.multiple_of((1 - core) * 1280 + t * 128, 128), 128)
            send_terms[pl.ds(pl.multiple_of(t * 128, 128), 128), :] = acc[place, :].astype(bf16)
        copy = red(0, 0, send_terms, half_in, core_peer())
        copy.start()
        return [copy]

    def reduce_x():
        @pl.loop(0, 10)
        def _(t):
            place = pl.ds(pl.multiple_of(t * 128, 128), 128)
            own = acc[pl.ds(pl.multiple_of(core * 1280 + t * 128, 128), 128), :]
            half_sum[place, :] = (own + half_in[place, :].astype(f32)).astype(bf16)
        copies = [red(1, n - 1, rows_at(half_sum, (xx + n) % 4 * 320, 320), quarter_in.at[n - 1], x_peer(n)) for n in (2, 1, 3)]
        for copy in copies:
            copy.start()
        return copies

    def reduce_z():
        own = rows_at(half_sum, xx * 320, 320)[...].astype(f32)
        for n in range(3):
            own += quarter_in[n].astype(f32)
        quarter_sum[...] = own.astype(bf16)
        copies = [red(2, n - 1, rows_at(quarter_sum, (zh + n) % 4 * 80, 80), last_in.at[n - 1], z_peer(n)) for n in (2, 1, 3)]
        for copy in copies:
            copy.start()
        return copies

    def gather_z():
        own = rows_at(quarter_sum, zh * 80, 80)[...].astype(f32)
        for n in range(3):
            own += last_in[n].astype(f32)
        place = rows_at(total, core * 1280 + xx * 320 + zh * 80, 80)
        place[...] = own.astype(bf16)
        copies = [red(3, n - 1, place, place, z_peer(n)) for n in (2, 1, 3)]
        for copy in copies:
            copy.start()
        return copies

    def gather_x():
        place = rows_at(total, core * 1280 + xx * 320, 320)
        copies = [red(4, n - 1, place, place, x_peer(n)) for n in (2, 1, 3)]
        for copy in copies:
            copy.start()
        return copies

    def gather_core():
        place = rows_at(total, core * 1280, 1280)
        copy = red(5, 0, place, place, core_peer())
        copy.start()
        return [copy]

    def finish(copies):
        for copy in copies:
            copy.wait()

    final = CHUNKS - 1
    for q in range(final):
        back_rows(q)
        seq_start(A3, q)
        last_terms(q)
    back_rows(final)
    last_terms(final)
    copies = reduce_core()
    seq_start(A3, final, (2,))
    out_rows(0)
    finish(copies)
    copies = reduce_x()
    seq_start(A3, final, (1, 3, 0))
    for q in range(1, CHUNKS):
        out_rows(q)
    for a in range(8):
        for half in range(2):
            out_v[a, :, half * 128 : half * 128 + 128] = wide[half, pl.ds(a, 256, stride=8), :].astype(bf16)
    stores = [pltpu.make_async_copy(out_v, out, store_sem.at[0])]
    stores[0].start()

    steps = [reduce_z, gather_z, gather_x, gather_core]
    for q in range(CHUNKS):
        seq_wait(A3, q)
        mix_columns(A3, A4, mix_bwd, q)
        parts = ((2, 1, 3, 0),) if q < final else ((2,), (1,), (3, 0))
        for part in parts:
            if steps:
                finish(copies)
                copies = steps.pop(0)()
            seq_start(A4, q, part)
    finish(copies)
    tall_v[0:256, :] = flip(total[0:256, :])
    tall_v[256:1280, :] = total[1280:2304, :]
    tall_v[1280:1536, :] = nn(unsort, total[2304:2560, :]).astype(bf16)
    for o in range(4):
        broad_v[:, o * 256 : o * 256 + 256] = nt(unsort, total[256 + o * 256 : 512 + o * 256, :]).astype(bf16)
    for n, (source, target) in enumerate(((tall_v, tall_out), (broad_v, broad_out))):
        stores.append(pltpu.make_async_copy(source, target, store_sem.at[n + 1]))
        stores[-1].start()

    for q in range(CHUNKS):
        seq_wait(A4, q)

        @pl.loop(0, 32)
        def _(d):
            for half in range(2):
                wide[half, block_place(d, q), :] = field_r[A4, q, d, :, half * 128 : half * 128 + 128].astype(f32)
    for a in range(8):
        lines = pl.ds(a, 256, stride=8)
        for half in range(2):
            twisted = (wide[half, lines, :] * tw[:, a : a + 1]).astype(bf16)
            grad_in[a, :, half * 128 : half * 128 + 128] = (extra[half, lines, :] + nn(mix_first[...], twisted)).astype(bf16)

    for store in stores:
        store.wait()
    for q in range(CHUNKS):
        for phase in range(4):
            sent = field_s.at[phase, q, pl.ds(0, 31)]
            pltpu.make_async_copy(sent, sent, seq_send.at[phase, q]).wait()
            sent = swap_s.at[phase, q, pl.ds(0, 224)]
            pltpu.make_async_copy(sent, sent, swap_send.at[phase, q]).wait()


def shards(activations, mix_first, twiddle, mix_second, up_first, up_second, down_first, down_second, grad_out):
    span = 2048 // CHUNKS
    args = (
        activations.reshape(8, 256, 256), mix_first, twiddle, grad_out.reshape(8, 256, 256), mix_second,
        up_first[0], up_second[0], down_first[0], down_second[0],
    )
    vmem = pl.BlockSpec(memory_space=pltpu.VMEM)
    rows = 64 // CHUNKS
    square = pltpu.VMEM((256, 256), bf16)
    broad, tall = pltpu.VMEM((256, 1024), bf16), pltpu.VMEM((1024, 256), bf16)
    output, tall_sums, broad_sums, grad_in = pl.pallas_call(
        layer,
        name="monarch_layer",
        out_shape=(
            jax.ShapeDtypeStruct((8, 256, 256), bf16),
            jax.ShapeDtypeStruct((1536, 256), bf16),
            jax.ShapeDtypeStruct((256, 1024), bf16),
            jax.ShapeDtypeStruct((8, 256, 256), bf16),
        ),
        in_specs=[vmem] * 3 + [pl.BlockSpec(memory_space=pl.ANY)] * 6,
        out_specs=(pl.BlockSpec(memory_space=pl.ANY),) * 3 + (vmem,),
        scratch_shapes=[
            pltpu.VMEM((8, 256, 256), bf16),
            square, square, broad, tall, square,
            pltpu.VMEM((CHUNKS, span, 256), bf16),
            pltpu.VMEM((CHUNKS, span, 256), bf16),
            square, square, broad, tall, broad, square,
            pltpu.VMEM((2560, 256), bf16),
            pltpu.VMEM((8, 256, 256), bf16),
            pltpu.VMEM((1536, 256), bf16),
            broad,
            pltpu.VMEM((2, 2048, 128), f32),
            pltpu.VMEM((2, 2048, 128), f32),
            pltpu.VMEM((4, CHUNKS, 32, rows, 256), bf16),
            pltpu.VMEM((4, CHUNKS, 32, rows, 256), bf16),
            pltpu.VMEM((4, CHUNKS, 256, span), bf16),
            pltpu.VMEM((4, CHUNKS, 256, span), bf16),
            pltpu.VMEM((CHUNKS, span, 256), bf16),
            pltpu.VMEM((CHUNKS, 1024, span), bf16),
            pltpu.VMEM((CHUNKS, 1024, span), bf16),
            pltpu.VMEM((2560, 256), f32),
            pltpu.VMEM((1280, 256), bf16),
            pltpu.VMEM((1280, 256), bf16),
            pltpu.VMEM((1280, 256), bf16),
            pltpu.VMEM((3, 320, 256), bf16),
            pltpu.VMEM((320, 256), bf16),
            pltpu.VMEM((3, 80, 256), bf16),
            pltpu.SemaphoreType.DMA((4, CHUNKS)),
            pltpu.SemaphoreType.DMA((4, CHUNKS)),
            pltpu.SemaphoreType.DMA((4, CHUNKS)),
            pltpu.SemaphoreType.DMA((4, CHUNKS)),
            pltpu.SemaphoreType.DMA((6, 3)),
            pltpu.SemaphoreType.DMA((6, 3)),
            pltpu.SemaphoreType.DMA((6,)),
            pltpu.SemaphoreType.DMA((3,)),
        ],
        compiler_params=pltpu.CompilerParams(collective_id=0, has_side_effects=True, vmem_limit_bytes=60 << 20),
    )(*args)

    tall_sums = tall_sums.astype(f32) * (1.0 / 256)
    broad_sums = broad_sums.astype(f32) * (1.0 / 256)
    return (
        output.reshape(2048, 256), grad_in.reshape(2048, 256),
        tall_sums[None, :256], broad_sums[None], tall_sums[None, 256:1280], tall_sums[None, 1280:],
    )


def solution(mesh):
    block = P("fsdp", None, None)
    in_specs = (P("seq", "fsdp"), P(), P("seq", None), P(), block, block, block, block, P("seq", "fsdp"))
    out_specs = (P("seq", "fsdp"), P("seq", "fsdp"), block, block, block, block)
    return jax.shard_map(shards, mesh=mesh, in_specs=in_specs, out_specs=out_specs, check_vma=False)
```

```python
import functools

import jax
import jax.numpy as jnp
from jax import lax
from jax.experimental import pallas as pl
from jax.experimental.pallas import tpu as pltpu
from jax.sharding import PartitionSpec as P

MESH = pl.DeviceIdType.MESH
bf16, f32 = jnp.bfloat16, jnp.float32
root_two_pi = 0.7978845608028654
cubic_term = 0.044715
CHUNKS = 4
A1, A2, A3, A4 = range(4)
BACK, UP, GRAD, DOWN = range(4)


def gelu_both(values):
    square = values * values
    hyper = jnp.tanh(root_two_pi * values * (1.0 + cubic_term * square))
    half = 0.5 * (1.0 + hyper)
    slope = half + 0.5 * values * (1.0 - hyper * hyper) * root_two_pi * (1.0 + 3.0 * cubic_term * square)
    return values * half, slope


def nn(left, right):
    return lax.dot_general(left, right, (((1,), (0,)), ((), ())), preferred_element_type=f32)


def nt(left, right):
    return lax.dot_general(left, right, (((1,), (1,)), ((), ())), preferred_element_type=f32)


def tn(left, right):
    return lax.dot_general(left, right, (((0,), (0,)), ((), ())), preferred_element_type=f32)


def layer(
    act_rows, mix_first, twiddle, gout_any, mix_second_any, first_any, second_any, third_any, fourth_any,
    out, tall_out, broad_out, grad_in,
    gout_rows, mix_bwd, first, second_raw, third, fourth_raw,
    act, gout, mix_fwd, first_t, second, second_t, third_t, fourth, total, out_v, tall_v, broad_v,
    wide, extra, field_s, field_r, swap_s, swap_r, hidden, active, gpre, acc, send_terms, half_in, half_sum,
    quarter_in, quarter_sum, last_in,
    seq_send, seq_recv, swap_send, swap_recv, red_send, red_recv, load_sem, store_sem,
):
    s = lax.axis_index("seq")
    f = lax.axis_index("fsdp")
    zh, xx, core = s // 8, (s // 2) % 4, s % 2
    zl, yy = f // 4, f % 4
    rows = field_s.shape[3]
    span = swap_s.shape[3]

    def seq_peer(dz, n):
        return ((zh + dz) % 4 * 4 + (xx + n // 2) % 4) * 2 + (core + n) % 2

    def swap_peer(n):
        return (zl + n // 4) % 2 * 4 + (yy + n) % 4

    barrier = pltpu.get_barrier_semaphore()

    def greet(peer_seq, peer_fsdp):
        pl.semaphore_signal(barrier, inc=1, device_id={"seq": peer_seq, "fsdp": peer_fsdp}, device_id_type=MESH)

    @pl.loop(1, 32)
    def _(n):
        greet((s + n) % 32, f)

    @pl.loop(1, 8)
    def _(n):
        greet(s, (f + n) % 8)

    def seq_start(phase, q, planes=(2, 1, 3, 0)):
        if 0 in planes:
            pltpu.make_async_copy(field_s.at[phase, q, s], field_r.at[phase, q, s], seq_recv.at[phase, q]).start()
        for dz in planes:
            @pl.loop(1 if dz == 0 else 0, 8, unroll=True)
            def _(n):
                peer = seq_peer(dz, n)
                pltpu.make_async_remote_copy(
                    src_ref=field_s.at[phase, q, peer], dst_ref=field_r.at[phase, q, s],
                    send_sem=seq_send.at[phase, q], recv_sem=seq_recv.at[phase, q],
                    device_id={"seq": peer, "fsdp": f}, device_id_type=MESH,
                ).start()

    def seq_wait(phase, q):
        whole = field_r.at[phase, q]
        pltpu.make_async_copy(whole, whole, seq_recv.at[phase, q]).wait()

    def swap_start(phase, q):
        own = pl.ds(pl.multiple_of(f * 32, 32), 32)
        pltpu.make_async_copy(swap_s.at[phase, q, own], swap_r.at[phase, q, own], swap_recv.at[phase, q]).start()

        @pl.loop(1, 8, unroll=True)
        def _(n):
            peer = swap_peer(8 - n)
            pltpu.make_async_remote_copy(
                src_ref=swap_s.at[phase, q, pl.ds(pl.multiple_of(peer * 32, 32), 32)], dst_ref=swap_r.at[phase, q, own],
                send_sem=swap_send.at[phase, q], recv_sem=swap_recv.at[phase, q],
                device_id={"seq": s, "fsdp": peer}, device_id_type=MESH,
            ).start()

    def swap_wait(phase, q):
        whole = swap_r.at[phase, q]
        pltpu.make_async_copy(whole, whole, swap_recv.at[phase, q]).wait()

    loads = [
        pltpu.make_async_copy(source, target, load_sem.at[index])
        for index, (source, target) in enumerate((
            (gout_any, gout_rows), (fourth_any, fourth_raw), (mix_second_any, mix_bwd),
            (first_any, first), (second_any, second_raw), (third_any, third),
        ))
    ]
    for load in loads:
        load.start()

    row = lax.broadcasted_iota(jnp.int32, (256, 256), 0)
    column = lax.broadcasted_iota(jnp.int32, (256, 256), 1)
    one, zero = jnp.ones((256, 256), f32), jnp.zeros((256, 256), f32)
    eye = jnp.where(row == column, one, zero).astype(bf16)
    sort = jnp.where(column == (row % 32) * 8 + row // 32, one, zero).astype(bf16)
    unsort = jnp.where(row == (column % 32) * 8 + column // 32, one, zero).astype(bf16)

    def flip(values):
        return nt(eye, values).astype(bf16)

    def halves(values):
        return [(half, values[:, half * 128 : half * 128 + 128]) for half in range(2)]

    def interleave(index, values):
        for half, part in halves(values):
            wide[half, pl.ds(index, 256, stride=8), :] = part

    def block_place(d, q):
        return pl.ds(pl.multiple_of(d * 64 + q * rows, 8), rows)

    tw = twiddle[...].T
    mix_in = flip(mix_first[...])
    for a in range(8):
        interleave(a, nn(mix_in, act_rows[a]) * tw[:, a : a + 1])
    for q in range(CHUNKS):
        @pl.loop(0, 32)
        def _(d):
            for half in range(2):
                field_s[A1, q, d, :, half * 128 : half * 128 + 128] = wide[half, block_place(d, q), :].astype(bf16)

    pl.semaphore_wait(barrier, 38)
    for q in range(CHUNKS):
        seq_start(A1, q)

    tile = 256
    tiles = span // tile
    per = tile // rows

    def token_tile(t):
        return pl.ds(pl.multiple_of(t * tile, tile), tile)

    def field_tile(ref, phase, q, t):
        return ref.at[phase, q, pl.ds(t * per, per)]

    def token_order(source, target):
        for a in range(8):
            interleave(a, source[a].astype(f32))
        for q in range(CHUNKS):
            @pl.loop(0, 32)
            def _(d):
                place = pl.ds(pl.multiple_of(d * rows, rows), rows)
                for half in range(2):
                    target[q, place, half * 128 : half * 128 + 128] = wide[half, block_place(d, q), :].astype(bf16)

    def scatter(target, q, t, values):
        for half, part in halves(values):
            for n in range(per):
                target[half, block_place(t * per + n, q), :] = part[n * rows : (n + 1) * rows]

    loads[0].wait()
    token_order(gout_rows, gout)
    loads[1].wait()
    fourth[...] = nn(sort, fourth_raw[...]).astype(bf16)
    for q in range(CHUNKS):
        @pl.loop(0, tiles)
        def _(t):
            swap_s[BACK, q, :, token_tile(t)] = nt(fourth[...], gout[q, token_tile(t), :]).astype(bf16)
        swap_start(BACK, q)
    token_order(act_rows, act)
    for load in loads[2:]:
        load.wait()
    mix_fwd[...] = flip(mix_bwd[...])
    first_t[...] = flip(first[...])
    for o in range(4):
        units = pl.ds(o * 256, 256)
        sorted_units = nn(sort, second_raw[:, units]).astype(bf16)
        second[:, units] = sorted_units
        second_t[units, :] = flip(sorted_units)
        third_t[:, units] = flip(third[units, :])

    def mix_columns(source, target, factor, q):
        for pair in range(rows // 16):
            part = pl.ds(pair * 16, 16)
            block = field_r[source, q, :, part, :].astype(f32).reshape(32, 2, 8, 256)
            mixed = [nn(factor[...], block[:, k].reshape(256, 256).astype(bf16)).reshape(32, 8, 256) for k in range(2)]
            field_s[target, q, :, part, :] = jnp.stack(mixed, axis=1).reshape(32, 16, 256).astype(bf16)

    def gate(q, t):
        return act[q, token_tile(t), :].astype(f32)

    for q in range(CHUNKS):
        seq_wait(A1, q)
        mix_columns(A1, A2, mix_fwd, q)
        seq_start(A2, q)

    for q in range(CHUNKS):
        seq_wait(A2, q)

        @pl.loop(0, tiles)
        def _(t):
            inputs = gate(q, t)
            mixed = field_tile(field_r, A2, q, t)[...].reshape(tile, 256).astype(f32)
            rows_hidden = (inputs + jax.nn.sigmoid(inputs) * mixed).astype(bf16)
            hidden[q, token_tile(t), :] = rows_hidden
            swap_s[UP, q, :, token_tile(t)] = nt(first_t[...], rows_hidden).astype(bf16)
        swap_start(UP, q)

    def add(place, values, q):
        if q == 0:
            acc[place, :] = values
        else:
            acc[place, :] += values

    for q in range(CHUNKS):
        if q == 0:
            for other in range(CHUNKS):
                swap_wait(BACK, other)
        swap_wait(UP, q)

        @pl.loop(0, tiles)
        def _(t):
            columns = token_tile(t)
            up = swap_r[UP, q, :, columns]
            back = swap_r[BACK, q, :, columns]

            @pl.loop(0, 4, unroll=True)
            def _(o):
                units = pl.ds(pl.multiple_of(o * 256, 256), 256)
                value, slope = gelu_both(nn(second_t[units, :], up))
                active[q, units, columns] = value.astype(bf16)
                gpre[q, units, columns] = (nn(third[units, :], back) * slope).astype(bf16)
            swap_s[GRAD, q, :, columns] = nn(second[...], gpre[q, :, columns]).astype(bf16)
        swap_start(GRAD, q)

        @pl.loop(0, tiles, unroll=True)
        def _(t):
            columns = token_tile(t)
            swap_s[DOWN, q, :, columns] = nn(third_t[...], active[q, :, columns]).astype(bf16)
        swap_start(DOWN, q)

        @pl.loop(0, 4, unroll=True)
        def _(o):
            units = pl.ds(pl.multiple_of(o * 256, 256), 256)
            add(pl.ds(pl.multiple_of(256 + o * 256, 256), 256), nt(gpre[q, units, :], swap_r[UP, q]), q)
            add(pl.ds(pl.multiple_of(1280 + o * 256, 256), 256), nt(active[q, units, :], swap_r[BACK, q]), q)

    def back_rows(q):
        swap_wait(GRAD, q)

        @pl.loop(0, tiles)
        def _(t):
            columns = token_tile(t)
            inner = tn(swap_r[GRAD, q, :, columns], first_t[...])
            back = (gout[q, columns, :].astype(f32) + inner).astype(bf16).astype(f32)
            gating = jax.nn.sigmoid(gate(q, t))
            mixed = field_tile(field_r, A2, q, t)[...].reshape(tile, 256).astype(f32)
            field_tile(field_s, A3, q, t)[...] = (back * gating).astype(bf16).reshape(per, rows, 256)
            rest = back * (1.0 + gating * (1.0 - gating) * mixed)
            scatter(extra, q, t, rest)

    def out_rows(q):
        @pl.loop(0, tiles)
        def _(t):
            columns = token_tile(t)
            scatter(wide, q, t, hidden[q, columns, :].astype(f32) + tn(swap_r[DOWN, q, :, columns], fourth[...]))

    def last_terms(q):
        add(pl.ds(0, 256), nn(swap_r[GRAD, q], hidden[q]), q)
        swap_wait(DOWN, q)
        add(pl.ds(2304, 256), nn(swap_r[DOWN, q], gout[q]), q)

    def core_peer():
        return {"seq": zh * 8 + xx * 2 + 1 - core, "fsdp": f}

    def x_peer(n):
        return {"seq": zh * 8 + (xx + n) % 4 * 2 + core, "fsdp": f}

    def z_peer(n):
        return {"seq": (zh + n) % 4 * 8 + xx * 2 + core, "fsdp": f}

    def red(stage, n, source, target, peer):
        return pltpu.make_async_remote_copy(
            src_ref=source, dst_ref=target, send_sem=red_send.at[stage, n], recv_sem=red_recv.at[stage, n],
            device_id=peer, device_id_type=MESH,
        )

    def rows_at(ref, start, count):
        return ref.at[pl.ds(pl.multiple_of(start, 16), count)]

    def reduce_core():
        @pl.loop(0, 10)
        def _(t):
            place = pl.ds(pl.multiple_of((1 - core) * 1280 + t * 128, 128), 128)
            send_terms[pl.ds(pl.multiple_of(t * 128, 128), 128), :] = acc[place, :].astype(bf16)
        copy = red(0, 0, send_terms, half_in, core_peer())
        copy.start()
        return [copy]

    def reduce_x():
        @pl.loop(0, 10)
        def _(t):
            place = pl.ds(pl.multiple_of(t * 128, 128), 128)
            own = acc[pl.ds(pl.multiple_of(core * 1280 + t * 128, 128), 128), :]
            half_sum[place, :] = (own + half_in[place, :].astype(f32)).astype(bf16)
        copies = [red(1, n - 1, rows_at(half_sum, (xx + n) % 4 * 320, 320), quarter_in.at[n - 1], x_peer(n)) for n in (2, 1, 3)]
        for copy in copies:
            copy.start()
        return copies

    def reduce_z():
        own = rows_at(half_sum, xx * 320, 320)[...].astype(f32)
        for n in range(3):
            own += quarter_in[n].astype(f32)
        quarter_sum[...] = own.astype(bf16)
        copies = [red(2, n - 1, rows_at(quarter_sum, (zh + n) % 4 * 80, 80), last_in.at[n - 1], z_peer(n)) for n in (2, 1, 3)]
        for copy in copies:
            copy.start()
        return copies

    def gather_z():
        own = rows_at(quarter_sum, zh * 80, 80)[...].astype(f32)
        for n in range(3):
            own += last_in[n].astype(f32)
        place = rows_at(total, core * 1280 + xx * 320 + zh * 80, 80)
        place[...] = own.astype(bf16)
        copies = [red(3, n - 1, place, place, z_peer(n)) for n in (2, 1, 3)]
        for copy in copies:
            copy.start()
        return copies

    def gather_x():
        place = rows_at(total, core * 1280 + xx * 320, 320)
        copies = [red(4, n - 1, place, place, x_peer(n)) for n in (2, 1, 3)]
        for copy in copies:
            copy.start()
        return copies

    def gather_core():
        place = rows_at(total, core * 1280, 1280)
        copy = red(5, 0, place, place, core_peer())
        copy.start()
        return [copy]

    def finish(copies):
        for copy in copies:
            copy.wait()

    final = CHUNKS - 1
    for q in range(final):
        back_rows(q)
        seq_start(A3, q)
        last_terms(q)
    back_rows(final)
    last_terms(final)
    copies = reduce_core()
    seq_start(A3, final, (2,))
    out_rows(0)
    finish(copies)
    copies = reduce_x()
    seq_start(A3, final, (1, 3, 0))
    for q in range(1, CHUNKS):
        out_rows(q)
    for a in range(8):
        for half in range(2):
            out_v[a, :, half * 128 : half * 128 + 128] = wide[half, pl.ds(a, 256, stride=8), :].astype(bf16)
    stores = [pltpu.make_async_copy(out_v, out, store_sem.at[0])]
    stores[0].start()

    steps = [reduce_z, gather_z, gather_x, gather_core]
    for q in range(CHUNKS):
        seq_wait(A3, q)
        mix_columns(A3, A4, mix_bwd, q)
        parts = ((2, 1, 3, 0),) if q < final else ((2,), (1,), (3, 0))
        for part in parts:
            if steps:
                finish(copies)
                copies = steps.pop(0)()
            seq_start(A4, q, part)
    finish(copies)
    tall_v[0:256, :] = flip(total[0:256, :])
    tall_v[256:1280, :] = total[1280:2304, :]
    tall_v[1280:1536, :] = nn(unsort, total[2304:2560, :]).astype(bf16)
    for o in range(4):
        broad_v[:, o * 256 : o * 256 + 256] = nt(unsort, total[256 + o * 256 : 512 + o * 256, :]).astype(bf16)
    for n, (source, target) in enumerate(((tall_v, tall_out), (broad_v, broad_out))):
        stores.append(pltpu.make_async_copy(source, target, store_sem.at[n + 1]))
        stores[-1].start()

    for q in range(CHUNKS):
        seq_wait(A4, q)

        @pl.loop(0, 32)
        def _(d):
            for half in range(2):
                wide[half, block_place(d, q), :] = field_r[A4, q, d, :, half * 128 : half * 128 + 128].astype(f32)
    for a in range(8):
        lines = pl.ds(a, 256, stride=8)
        for half in range(2):
            twisted = (wide[half, lines, :] * tw[:, a : a + 1]).astype(bf16)
            grad_in[a, :, half * 128 : half * 128 + 128] = (extra[half, lines, :] + nn(mix_first[...], twisted)).astype(bf16)

    for store in stores:
        store.wait()
    for q in range(CHUNKS):
        for phase in range(4):
            sent = field_s.at[phase, q, pl.ds(0, 31)]
            pltpu.make_async_copy(sent, sent, seq_send.at[phase, q]).wait()
            sent = swap_s.at[phase, q, pl.ds(0, 224)]
            pltpu.make_async_copy(sent, sent, swap_send.at[phase, q]).wait()


def hand_out(
    rows_in, grad_in, tall_in, broad_in, rows_out, grad_out, first, second, third, fourth,
    rows_v, grad_v, tall_v, broad_v, tall_f, broad_f, load_sem, store_sem,
):
    loads = [
        pltpu.make_async_copy(source, target, load_sem.at[n])
        for n, (source, target) in enumerate(((tall_in, tall_v), (broad_in, broad_v), (rows_in, rows_v), (grad_in, grad_v)))
    ]
    for load in loads:
        load.start()
    stores = []

    def store(source, target):
        stores.append(pltpu.make_async_copy(source, target, store_sem.at[len(stores)]))
        stores[-1].start()

    scale = 1.0 / 256
    loads[0].wait()
    tall_f[...] = tall_v[...].astype(f32) * scale
    store(tall_f.at[pl.ds(0, 256)], first)
    store(tall_f.at[pl.ds(256, 1024)], third)
    store(tall_f.at[pl.ds(1280, 256)], fourth)
    loads[1].wait()
    broad_f[...] = broad_v[...].astype(f32) * scale
    store(broad_f, second)
    loads[2].wait()
    store(rows_v, rows_out)
    loads[3].wait()
    store(grad_v, grad_out)
    for copy in stores:
        copy.wait()


def shards(activations, mix_first, twiddle, mix_second, up_first, up_second, down_first, down_second, grad_out):
    span = 2048 // CHUNKS
    args = (
        activations.reshape(8, 256, 256), mix_first, twiddle, grad_out.reshape(8, 256, 256), mix_second,
        up_first[0], up_second[0], down_first[0], down_second[0],
    )
    vmem = pl.BlockSpec(memory_space=pltpu.VMEM)
    rows = 64 // CHUNKS
    square = pltpu.VMEM((256, 256), bf16)
    broad, tall = pltpu.VMEM((256, 1024), bf16), pltpu.VMEM((1024, 256), bf16)
    output, tall_sums, broad_sums, grad_in = pl.pallas_call(
        layer,
        name="monarch_layer",
        out_shape=(
            jax.ShapeDtypeStruct((8, 256, 256), bf16),
            jax.ShapeDtypeStruct((1536, 256), bf16),
            jax.ShapeDtypeStruct((256, 1024), bf16),
            jax.ShapeDtypeStruct((8, 256, 256), bf16),
        ),
        in_specs=[vmem] * 3 + [pl.BlockSpec(memory_space=pl.ANY)] * 6,
        out_specs=(pl.BlockSpec(memory_space=pl.ANY),) * 3 + (vmem,),
        scratch_shapes=[
            pltpu.VMEM((8, 256, 256), bf16),
            square, square, broad, tall, square,
            pltpu.VMEM((CHUNKS, span, 256), bf16),
            pltpu.VMEM((CHUNKS, span, 256), bf16),
            square, square, broad, tall, broad, square,
            pltpu.VMEM((2560, 256), bf16),
            pltpu.VMEM((8, 256, 256), bf16),
            pltpu.VMEM((1536, 256), bf16),
            broad,
            pltpu.VMEM((2, 2048, 128), f32),
            pltpu.VMEM((2, 2048, 128), f32),
            pltpu.VMEM((4, CHUNKS, 32, rows, 256), bf16),
            pltpu.VMEM((4, CHUNKS, 32, rows, 256), bf16),
            pltpu.VMEM((4, CHUNKS, 256, span), bf16),
            pltpu.VMEM((4, CHUNKS, 256, span), bf16),
            pltpu.VMEM((CHUNKS, span, 256), bf16),
            pltpu.VMEM((CHUNKS, 1024, span), bf16),
            pltpu.VMEM((CHUNKS, 1024, span), bf16),
            pltpu.VMEM((2560, 256), f32),
            pltpu.VMEM((1280, 256), bf16),
            pltpu.VMEM((1280, 256), bf16),
            pltpu.VMEM((1280, 256), bf16),
            pltpu.VMEM((3, 320, 256), bf16),
            pltpu.VMEM((320, 256), bf16),
            pltpu.VMEM((3, 80, 256), bf16),
            pltpu.SemaphoreType.DMA((4, CHUNKS)),
            pltpu.SemaphoreType.DMA((4, CHUNKS)),
            pltpu.SemaphoreType.DMA((4, CHUNKS)),
            pltpu.SemaphoreType.DMA((4, CHUNKS)),
            pltpu.SemaphoreType.DMA((6, 3)),
            pltpu.SemaphoreType.DMA((6, 3)),
            pltpu.SemaphoreType.DMA((6,)),
            pltpu.SemaphoreType.DMA((3,)),
        ],
        compiler_params=pltpu.CompilerParams(collective_id=0, has_side_effects=True, vmem_limit_bytes=60 << 20),
    )(*args)

    anywhere = pl.BlockSpec(memory_space=pl.ANY)
    output, grad_in, sum_first, sum_second, sum_third, sum_fourth = pl.pallas_call(
        hand_out,
        name="hand_out",
        out_shape=(
            jax.ShapeDtypeStruct((8, 256, 256), bf16),
            jax.ShapeDtypeStruct((8, 256, 256), bf16),
            jax.ShapeDtypeStruct((256, 256), f32),
            jax.ShapeDtypeStruct((256, 1024), f32),
            jax.ShapeDtypeStruct((1024, 256), f32),
            jax.ShapeDtypeStruct((256, 256), f32),
        ),
        in_specs=[anywhere] * 4,
        out_specs=(anywhere,) * 6,
        scratch_shapes=[
            pltpu.VMEM((8, 256, 256), bf16),
            pltpu.VMEM((8, 256, 256), bf16),
            pltpu.VMEM((1536, 256), bf16),
            broad,
            pltpu.VMEM((1536, 256), f32),
            pltpu.VMEM((256, 1024), f32),
            pltpu.SemaphoreType.DMA((4,)),
            pltpu.SemaphoreType.DMA((6,)),
        ],
        compiler_params=pltpu.CompilerParams(vmem_limit_bytes=60 << 20),
    )(output, grad_in, tall_sums, broad_sums)
    return (
        output.reshape(2048, 256), grad_in.reshape(2048, 256),
        sum_first[None], sum_second[None], sum_third[None], sum_fourth[None],
    )


def solution(mesh):
    block = P("fsdp", None, None)
    in_specs = (P("seq", "fsdp"), P(), P("seq", None), P(), block, block, block, block, P("seq", "fsdp"))
    out_specs = (P("seq", "fsdp"), P("seq", "fsdp"), block, block, block, block)
    return jax.shard_map(shards, mesh=mesh, in_specs=in_specs, out_specs=out_specs, check_vma=False)
```

```python
import functools

import jax
import jax.numpy as jnp
from jax import lax
from jax.experimental import pallas as pl
from jax.experimental.pallas import tpu as pltpu
from jax.sharding import PartitionSpec as P

MESH = pl.DeviceIdType.MESH
bf16, f32 = jnp.bfloat16, jnp.float32
root_two_pi = 0.7978845608028654
cubic_term = 0.044715
CHUNKS = 4
A1, A2, A3, A4 = range(4)
BACK, UP, GRAD, DOWN = range(4)


def gelu_both(values):
    square = values * values
    hyper = jnp.tanh(root_two_pi * values * (1.0 + cubic_term * square))
    half = 0.5 * (1.0 + hyper)
    slope = half + 0.5 * values * (1.0 - hyper * hyper) * root_two_pi * (1.0 + 3.0 * cubic_term * square)
    return values * half, slope


def nn(left, right):
    return lax.dot_general(left, right, (((1,), (0,)), ((), ())), preferred_element_type=f32)


def nt(left, right):
    return lax.dot_general(left, right, (((1,), (1,)), ((), ())), preferred_element_type=f32)


def tn(left, right):
    return lax.dot_general(left, right, (((0,), (0,)), ((), ())), preferred_element_type=f32)


def layer(
    act_rows, mix_first, twiddle, gout_any, mix_second_any, first_any, second_any, third_any, fourth_any,
    out, tall_out, broad_out, grad_in,
    gout_rows, mix_bwd, first, second_raw, third, fourth_raw,
    act, gout, mix_fwd, first_t, second, second_t, third_t, fourth, total, out_v, tall_v, broad_v,
    wide, extra, field_s, field_r, swap_s, swap_r, hidden, active, gpre, acc, send_terms, half_in, half_sum,
    quarter_in, quarter_sum, last_in,
    seq_send, seq_recv, swap_send, swap_recv, red_send, red_recv, load_sem, store_sem,
):
    s = lax.axis_index("seq")
    f = lax.axis_index("fsdp")
    zh, xx, core = s // 8, (s // 2) % 4, s % 2
    zl, yy = f // 4, f % 4
    rows = field_s.shape[3]
    span = swap_s.shape[3]

    def seq_peer(dz, n):
        return ((zh + dz) % 4 * 4 + (xx + n // 2) % 4) * 2 + (core + n) % 2

    def swap_peer(n):
        return (zl + n // 4) % 2 * 4 + (yy + n) % 4

    barrier = pltpu.get_barrier_semaphore()

    def greet(peer_seq, peer_fsdp):
        pl.semaphore_signal(barrier, inc=1, device_id={"seq": peer_seq, "fsdp": peer_fsdp}, device_id_type=MESH)

    @pl.loop(1, 32)
    def _(n):
        greet((s + n) % 32, f)

    @pl.loop(1, 8)
    def _(n):
        greet(s, (f + n) % 8)

    def seq_start(phase, q, planes=(2, 1, 3, 0)):
        if 0 in planes:
            pltpu.make_async_copy(field_s.at[phase, q, s], field_r.at[phase, q, s], seq_recv.at[phase, q]).start()
        def send(dz, n):
            peer = seq_peer(dz, n)
            pltpu.make_async_remote_copy(
                src_ref=field_s.at[phase, q, peer], dst_ref=field_r.at[phase, q, s],
                send_sem=seq_send.at[phase, q], recv_sem=seq_recv.at[phase, q],
                device_id={"seq": peer, "fsdp": f}, device_id_type=MESH,
            ).start()

        for dz in planes:
            if dz:
                send(dz, 0)

        @pl.loop(1, 8, unroll=True)
        def _(n):
            for dz in planes:
                send(dz, n)

    def seq_wait(phase, q):
        whole = field_r.at[phase, q]
        pltpu.make_async_copy(whole, whole, seq_recv.at[phase, q]).wait()

    def swap_start(phase, q):
        own = pl.ds(pl.multiple_of(f * 32, 32), 32)
        pltpu.make_async_copy(swap_s.at[phase, q, own], swap_r.at[phase, q, own], swap_recv.at[phase, q]).start()

        @pl.loop(1, 8, unroll=True)
        def _(n):
            peer = swap_peer(8 - n)
            pltpu.make_async_remote_copy(
                src_ref=swap_s.at[phase, q, pl.ds(pl.multiple_of(peer * 32, 32), 32)], dst_ref=swap_r.at[phase, q, own],
                send_sem=swap_send.at[phase, q], recv_sem=swap_recv.at[phase, q],
                device_id={"seq": s, "fsdp": peer}, device_id_type=MESH,
            ).start()

    def swap_wait(phase, q):
        whole = swap_r.at[phase, q]
        pltpu.make_async_copy(whole, whole, swap_recv.at[phase, q]).wait()

    loads = [
        pltpu.make_async_copy(source, target, load_sem.at[index])
        for index, (source, target) in enumerate((
            (gout_any, gout_rows), (fourth_any, fourth_raw), (mix_second_any, mix_bwd),
            (first_any, first), (second_any, second_raw), (third_any, third),
        ))
    ]
    for load in loads:
        load.start()

    row = lax.broadcasted_iota(jnp.int32, (256, 256), 0)
    column = lax.broadcasted_iota(jnp.int32, (256, 256), 1)
    one, zero = jnp.ones((256, 256), f32), jnp.zeros((256, 256), f32)
    eye = jnp.where(row == column, one, zero).astype(bf16)
    sort = jnp.where(column == (row % 32) * 8 + row // 32, one, zero).astype(bf16)
    unsort = jnp.where(row == (column % 32) * 8 + column // 32, one, zero).astype(bf16)

    def flip(values):
        return nt(eye, values).astype(bf16)

    def halves(values):
        return [(half, values[:, half * 128 : half * 128 + 128]) for half in range(2)]

    def interleave(index, values):
        for half, part in halves(values):
            wide[half, pl.ds(index, 256, stride=8), :] = part

    def block_place(d, q):
        return pl.ds(pl.multiple_of(d * 64 + q * rows, 8), rows)

    tw = twiddle[...].T
    mix_in = flip(mix_first[...])
    for a in range(8):
        interleave(a, nn(mix_in, act_rows[a]) * tw[:, a : a + 1])
    for q in range(CHUNKS):
        @pl.loop(0, 32)
        def _(d):
            for half in range(2):
                field_s[A1, q, d, :, half * 128 : half * 128 + 128] = wide[half, block_place(d, q), :].astype(bf16)

    pl.semaphore_wait(barrier, 38)
    for q in range(CHUNKS):
        seq_start(A1, q)

    tile = 256
    tiles = span // tile
    per = tile // rows

    def token_tile(t):
        return pl.ds(pl.multiple_of(t * tile, tile), tile)

    def field_tile(ref, phase, q, t):
        return ref.at[phase, q, pl.ds(t * per, per)]

    def token_order(source, target):
        for a in range(8):
            interleave(a, source[a].astype(f32))
        for q in range(CHUNKS):
            @pl.loop(0, 32)
            def _(d):
                place = pl.ds(pl.multiple_of(d * rows, rows), rows)
                for half in range(2):
                    target[q, place, half * 128 : half * 128 + 128] = wide[half, block_place(d, q), :].astype(bf16)

    def scatter(target, q, t, values):
        for half, part in halves(values):
            for n in range(per):
                target[half, block_place(t * per + n, q), :] = part[n * rows : (n + 1) * rows]

    loads[0].wait()
    token_order(gout_rows, gout)
    loads[1].wait()
    fourth[...] = nn(sort, fourth_raw[...]).astype(bf16)
    for q in range(CHUNKS):
        @pl.loop(0, tiles)
        def _(t):
            swap_s[BACK, q, :, token_tile(t)] = nt(fourth[...], gout[q, token_tile(t), :]).astype(bf16)
        swap_start(BACK, q)
    token_order(act_rows, act)
    for load in loads[2:]:
        load.wait()
    mix_fwd[...] = flip(mix_bwd[...])
    first_t[...] = flip(first[...])
    for o in range(4):
        units = pl.ds(o * 256, 256)
        sorted_units = nn(sort, second_raw[:, units]).astype(bf16)
        second[:, units] = sorted_units
        second_t[units, :] = flip(sorted_units)
        third_t[:, units] = flip(third[units, :])

    def mix_columns(source, target, factor, q):
        for pair in range(rows // 16):
            part = pl.ds(pair * 16, 16)
            block = field_r[source, q, :, part, :].astype(f32).reshape(32, 2, 8, 256)
            mixed = [nn(factor[...], block[:, k].reshape(256, 256).astype(bf16)).reshape(32, 8, 256) for k in range(2)]
            field_s[target, q, :, part, :] = jnp.stack(mixed, axis=1).reshape(32, 16, 256).astype(bf16)

    def gate(q, t):
        return act[q, token_tile(t), :].astype(f32)

    for q in range(CHUNKS):
        seq_wait(A1, q)
        mix_columns(A1, A2, mix_fwd, q)
        seq_start(A2, q)

    for q in range(CHUNKS):
        seq_wait(A2, q)

        @pl.loop(0, tiles)
        def _(t):
            inputs = gate(q, t)
            mixed = field_tile(field_r, A2, q, t)[...].reshape(tile, 256).astype(f32)
            rows_hidden = (inputs + jax.nn.sigmoid(inputs) * mixed).astype(bf16)
            hidden[q, token_tile(t), :] = rows_hidden
            swap_s[UP, q, :, token_tile(t)] = nt(first_t[...], rows_hidden).astype(bf16)
        swap_start(UP, q)

    def add(place, values, q):
        if q == 0:
            acc[place, :] = values
        else:
            acc[place, :] += values

    for q in range(CHUNKS):
        if q == 0:
            for other in range(CHUNKS):
                swap_wait(BACK, other)
        swap_wait(UP, q)

        @pl.loop(0, tiles)
        def _(t):
            columns = token_tile(t)
            up = swap_r[UP, q, :, columns]
            back = swap_r[BACK, q, :, columns]

            @pl.loop(0, 4, unroll=True)
            def _(o):
                units = pl.ds(pl.multiple_of(o * 256, 256), 256)
                value, slope = gelu_both(nn(second_t[units, :], up))
                active[q, units, columns] = value.astype(bf16)
                gpre[q, units, columns] = (nn(third[units, :], back) * slope).astype(bf16)
            swap_s[GRAD, q, :, columns] = nn(second[...], gpre[q, :, columns]).astype(bf16)
        swap_start(GRAD, q)

        @pl.loop(0, tiles, unroll=True)
        def _(t):
            columns = token_tile(t)
            swap_s[DOWN, q, :, columns] = nn(third_t[...], active[q, :, columns]).astype(bf16)
        swap_start(DOWN, q)

        @pl.loop(0, 4, unroll=True)
        def _(o):
            units = pl.ds(pl.multiple_of(o * 256, 256), 256)
            add(pl.ds(pl.multiple_of(256 + o * 256, 256), 256), nt(gpre[q, units, :], swap_r[UP, q]), q)
            add(pl.ds(pl.multiple_of(1280 + o * 256, 256), 256), nt(active[q, units, :], swap_r[BACK, q]), q)

    def back_rows(q):
        swap_wait(GRAD, q)

        @pl.loop(0, tiles)
        def _(t):
            columns = token_tile(t)
            inner = tn(swap_r[GRAD, q, :, columns], first_t[...])
            back = (gout[q, columns, :].astype(f32) + inner).astype(bf16).astype(f32)
            gating = jax.nn.sigmoid(gate(q, t))
            mixed = field_tile(field_r, A2, q, t)[...].reshape(tile, 256).astype(f32)
            field_tile(field_s, A3, q, t)[...] = (back * gating).astype(bf16).reshape(per, rows, 256)
            rest = back * (1.0 + gating * (1.0 - gating) * mixed)
            scatter(extra, q, t, rest)

    def out_rows(q):
        @pl.loop(0, tiles)
        def _(t):
            columns = token_tile(t)
            scatter(wide, q, t, hidden[q, columns, :].astype(f32) + tn(swap_r[DOWN, q, :, columns], fourth[...]))

    def last_terms(q):
        add(pl.ds(0, 256), nn(swap_r[GRAD, q], hidden[q]), q)
        swap_wait(DOWN, q)
        add(pl.ds(2304, 256), nn(swap_r[DOWN, q], gout[q]), q)

    def core_peer():
        return {"seq": zh * 8 + xx * 2 + 1 - core, "fsdp": f}

    def x_peer(n):
        return {"seq": zh * 8 + (xx + n) % 4 * 2 + core, "fsdp": f}

    def z_peer(n):
        return {"seq": (zh + n) % 4 * 8 + xx * 2 + core, "fsdp": f}

    def red(stage, n, source, target, peer):
        return pltpu.make_async_remote_copy(
            src_ref=source, dst_ref=target, send_sem=red_send.at[stage, n], recv_sem=red_recv.at[stage, n],
            device_id=peer, device_id_type=MESH,
        )

    def rows_at(ref, start, count):
        return ref.at[pl.ds(pl.multiple_of(start, 16), count)]

    def reduce_core():
        @pl.loop(0, 10)
        def _(t):
            place = pl.ds(pl.multiple_of((1 - core) * 1280 + t * 128, 128), 128)
            send_terms[pl.ds(pl.multiple_of(t * 128, 128), 128), :] = acc[place, :].astype(bf16)
        copy = red(0, 0, send_terms, half_in, core_peer())
        copy.start()
        return [copy]

    def reduce_x():
        @pl.loop(0, 10)
        def _(t):
            place = pl.ds(pl.multiple_of(t * 128, 128), 128)
            own = acc[pl.ds(pl.multiple_of(core * 1280 + t * 128, 128), 128), :]
            half_sum[place, :] = (own + half_in[place, :].astype(f32)).astype(bf16)
        copies = [red(1, n - 1, rows_at(half_sum, (xx + n) % 4 * 320, 320), quarter_in.at[n - 1], x_peer(n)) for n in (2, 1, 3)]
        for copy in copies:
            copy.start()
        return copies

    def reduce_z():
        own = rows_at(half_sum, xx * 320, 320)[...].astype(f32)
        for n in range(3):
            own += quarter_in[n].astype(f32)
        quarter_sum[...] = own.astype(bf16)
        copies = [red(2, n - 1, rows_at(quarter_sum, (zh + n) % 4 * 80, 80), last_in.at[n - 1], z_peer(n)) for n in (2, 1, 3)]
        for copy in copies:
            copy.start()
        return copies

    def gather_z():
        own = rows_at(quarter_sum, zh * 80, 80)[...].astype(f32)
        for n in range(3):
            own += last_in[n].astype(f32)
        place = rows_at(total, core * 1280 + xx * 320 + zh * 80, 80)
        place[...] = own.astype(bf16)
        copies = [red(3, n - 1, place, place, z_peer(n)) for n in (2, 1, 3)]
        for copy in copies:
            copy.start()
        return copies

    def gather_x():
        place = rows_at(total, core * 1280 + xx * 320, 320)
        copies = [red(4, n - 1, place, place, x_peer(n)) for n in (2, 1, 3)]
        for copy in copies:
            copy.start()
        return copies

    def gather_core():
        place = rows_at(total, core * 1280, 1280)
        copy = red(5, 0, place, place, core_peer())
        copy.start()
        return [copy]

    def finish(copies):
        for copy in copies:
            copy.wait()

    final = CHUNKS - 1
    for q in range(final):
        back_rows(q)
        seq_start(A3, q)
        last_terms(q)
    back_rows(final)
    last_terms(final)
    copies = reduce_core()
    seq_start(A3, final, (2,))
    out_rows(0)
    finish(copies)
    copies = reduce_x()
    seq_start(A3, final, (1, 3, 0))
    for q in range(1, CHUNKS):
        out_rows(q)
    for a in range(8):
        for half in range(2):
            out_v[a, :, half * 128 : half * 128 + 128] = wide[half, pl.ds(a, 256, stride=8), :].astype(bf16)
    stores = [pltpu.make_async_copy(out_v, out, store_sem.at[0])]
    stores[0].start()

    steps = [reduce_z, gather_z, gather_x, gather_core]
    for q in range(CHUNKS):
        seq_wait(A3, q)
        mix_columns(A3, A4, mix_bwd, q)
        parts = ((2, 1, 3, 0),) if q < final else ((2,), (1,), (3, 0))
        for part in parts:
            if steps:
                finish(copies)
                copies = steps.pop(0)()
            seq_start(A4, q, part)
    finish(copies)
    tall_v[0:256, :] = flip(total[0:256, :])
    tall_v[256:1280, :] = total[1280:2304, :]
    tall_v[1280:1536, :] = nn(unsort, total[2304:2560, :]).astype(bf16)
    for o in range(4):
        broad_v[:, o * 256 : o * 256 + 256] = nt(unsort, total[256 + o * 256 : 512 + o * 256, :]).astype(bf16)
    for n, (source, target) in enumerate(((tall_v, tall_out), (broad_v, broad_out))):
        stores.append(pltpu.make_async_copy(source, target, store_sem.at[n + 1]))
        stores[-1].start()

    for q in range(CHUNKS):
        seq_wait(A4, q)

        @pl.loop(0, 32)
        def _(d):
            for half in range(2):
                wide[half, block_place(d, q), :] = field_r[A4, q, d, :, half * 128 : half * 128 + 128].astype(f32)
    for a in range(8):
        lines = pl.ds(a, 256, stride=8)
        for half in range(2):
            twisted = (wide[half, lines, :] * tw[:, a : a + 1]).astype(bf16)
            grad_in[a, :, half * 128 : half * 128 + 128] = (extra[half, lines, :] + nn(mix_first[...], twisted)).astype(bf16)

    for store in stores:
        store.wait()
    for q in range(CHUNKS):
        for phase in range(4):
            sent = field_s.at[phase, q, pl.ds(0, 31)]
            pltpu.make_async_copy(sent, sent, seq_send.at[phase, q]).wait()
            sent = swap_s.at[phase, q, pl.ds(0, 224)]
            pltpu.make_async_copy(sent, sent, swap_send.at[phase, q]).wait()


def hand_out(
    rows_in, grad_in, tall_in, broad_in, rows_out, grad_out, first, second, third, fourth,
    rows_v, grad_v, tall_v, broad_v, tall_f, broad_f, load_sem, store_sem,
):
    loads = [
        pltpu.make_async_copy(source, target, load_sem.at[n])
        for n, (source, target) in enumerate(((tall_in, tall_v), (broad_in, broad_v), (rows_in, rows_v), (grad_in, grad_v)))
    ]
    for load in loads:
        load.start()
    stores = []

    def store(source, target):
        stores.append(pltpu.make_async_copy(source, target, store_sem.at[len(stores)]))
        stores[-1].start()

    scale = 1.0 / 256
    loads[0].wait()
    tall_f[...] = tall_v[...].astype(f32) * scale
    store(tall_f.at[pl.ds(0, 256)], first)
    store(tall_f.at[pl.ds(256, 1024)], third)
    store(tall_f.at[pl.ds(1280, 256)], fourth)
    loads[1].wait()
    broad_f[...] = broad_v[...].astype(f32) * scale
    store(broad_f, second)
    loads[2].wait()
    store(rows_v, rows_out)
    loads[3].wait()
    store(grad_v, grad_out)
    for copy in stores:
        copy.wait()


def shards(activations, mix_first, twiddle, mix_second, up_first, up_second, down_first, down_second, grad_out):
    span = 2048 // CHUNKS
    args = (
        activations.reshape(8, 256, 256), mix_first, twiddle, grad_out.reshape(8, 256, 256), mix_second,
        up_first[0], up_second[0], down_first[0], down_second[0],
    )
    vmem = pl.BlockSpec(memory_space=pltpu.VMEM)
    rows = 64 // CHUNKS
    square = pltpu.VMEM((256, 256), bf16)
    broad, tall = pltpu.VMEM((256, 1024), bf16), pltpu.VMEM((1024, 256), bf16)
    output, tall_sums, broad_sums, grad_in = pl.pallas_call(
        layer,
        name="monarch_layer",
        out_shape=(
            jax.ShapeDtypeStruct((8, 256, 256), bf16),
            jax.ShapeDtypeStruct((1536, 256), bf16),
            jax.ShapeDtypeStruct((256, 1024), bf16),
            jax.ShapeDtypeStruct((8, 256, 256), bf16),
        ),
        in_specs=[vmem] * 3 + [pl.BlockSpec(memory_space=pl.ANY)] * 6,
        out_specs=(pl.BlockSpec(memory_space=pl.ANY),) * 3 + (vmem,),
        scratch_shapes=[
            pltpu.VMEM((8, 256, 256), bf16),
            square, square, broad, tall, square,
            pltpu.VMEM((CHUNKS, span, 256), bf16),
            pltpu.VMEM((CHUNKS, span, 256), bf16),
            square, square, broad, tall, broad, square,
            pltpu.VMEM((2560, 256), bf16),
            pltpu.VMEM((8, 256, 256), bf16),
            pltpu.VMEM((1536, 256), bf16),
            broad,
            pltpu.VMEM((2, 2048, 128), f32),
            pltpu.VMEM((2, 2048, 128), f32),
            pltpu.VMEM((4, CHUNKS, 32, rows, 256), bf16),
            pltpu.VMEM((4, CHUNKS, 32, rows, 256), bf16),
            pltpu.VMEM((4, CHUNKS, 256, span), bf16),
            pltpu.VMEM((4, CHUNKS, 256, span), bf16),
            pltpu.VMEM((CHUNKS, span, 256), bf16),
            pltpu.VMEM((CHUNKS, 1024, span), bf16),
            pltpu.VMEM((CHUNKS, 1024, span), bf16),
            pltpu.VMEM((2560, 256), f32),
            pltpu.VMEM((1280, 256), bf16),
            pltpu.VMEM((1280, 256), bf16),
            pltpu.VMEM((1280, 256), bf16),
            pltpu.VMEM((3, 320, 256), bf16),
            pltpu.VMEM((320, 256), bf16),
            pltpu.VMEM((3, 80, 256), bf16),
            pltpu.SemaphoreType.DMA((4, CHUNKS)),
            pltpu.SemaphoreType.DMA((4, CHUNKS)),
            pltpu.SemaphoreType.DMA((4, CHUNKS)),
            pltpu.SemaphoreType.DMA((4, CHUNKS)),
            pltpu.SemaphoreType.DMA((6, 3)),
            pltpu.SemaphoreType.DMA((6, 3)),
            pltpu.SemaphoreType.DMA((6,)),
            pltpu.SemaphoreType.DMA((3,)),
        ],
        compiler_params=pltpu.CompilerParams(collective_id=0, has_side_effects=True, vmem_limit_bytes=60 << 20),
    )(*args)

    anywhere = pl.BlockSpec(memory_space=pl.ANY)
    output, grad_in, sum_first, sum_second, sum_third, sum_fourth = pl.pallas_call(
        hand_out,
        name="hand_out",
        out_shape=(
            jax.ShapeDtypeStruct((8, 256, 256), bf16),
            jax.ShapeDtypeStruct((8, 256, 256), bf16),
            jax.ShapeDtypeStruct((256, 256), f32),
            jax.ShapeDtypeStruct((256, 1024), f32),
            jax.ShapeDtypeStruct((1024, 256), f32),
            jax.ShapeDtypeStruct((256, 256), f32),
        ),
        in_specs=[anywhere] * 4,
        out_specs=(anywhere,) * 6,
        scratch_shapes=[
            pltpu.VMEM((8, 256, 256), bf16),
            pltpu.VMEM((8, 256, 256), bf16),
            pltpu.VMEM((1536, 256), bf16),
            broad,
            pltpu.VMEM((1536, 256), f32),
            pltpu.VMEM((256, 1024), f32),
            pltpu.SemaphoreType.DMA((4,)),
            pltpu.SemaphoreType.DMA((6,)),
        ],
        compiler_params=pltpu.CompilerParams(vmem_limit_bytes=60 << 20),
    )(output, grad_in, tall_sums, broad_sums)
    return (
        output.reshape(2048, 256), grad_in.reshape(2048, 256),
        sum_first[None], sum_second[None], sum_third[None], sum_fourth[None],
    )


def solution(mesh):
    block = P("fsdp", None, None)
    in_specs = (P("seq", "fsdp"), P(), P("seq", None), P(), block, block, block, block, P("seq", "fsdp"))
    out_specs = (P("seq", "fsdp"), P("seq", "fsdp"), block, block, block, block)
    return jax.shard_map(shards, mesh=mesh, in_specs=in_specs, out_specs=out_specs, check_vma=False)
```
